512 devices in a mesh: ens: 16 (over y, core), lat: 32 (over x, z).
Axes of the slice: x: 4, y: 8, z: 8, core: 2. Of those that a mesh axis runs over, the one named last changes fastest.
Arguments:
- members: bfloat16 [16, 64, 384, 720], P('ens', None, 'lat'), may hold values from -6 to 6
- analysis: bfloat16 [64, 384, 720], P(None, 'lat'), may hold values from -6 to 6
- wave_order: int32 [320], replicated, may hold values from 0 to 319, each once
Outputs:
- grid_grad: bfloat16 [16, 64, 384, 720], P('ens', None, 'lat')
- coef_score: float32 [320, 320], P('lat', 'ens')
The draws below stay inside these ranges and needn't reach their ends.
Inputs may be any that keep to these rules, and one draw needn't show every extreme that they name: wave_order names each wavenumber from 0 to 319 exactly once.
All inputs are finite; a program needn't handle non-finite values.
Results may differ from the reference program's by a relative error of at most 0.014.
The reference program's roundings to bfloat16 on the way (of `deviation`, `fourier_table`, `fourier`, `legendre`, `spectra`, `coef_grad` and `returned`) count: a program that leaves them out, or rounds other values in their place, can miss the bound.
Values may be sent and summed in bfloat16 or wider, within the bound.
No kernel may reach another device: no remote copies, remote signals or barrier semaphores. Data moves between devices by JAX's collectives and lax.ppermute only.
A program may use at most 128 MiB of HBM per device.

```python
import math
import jax
import jax.numpy as jnp
from jax import lax

VARS = 64
M = 320
NLON = 720
NLAT = 384
L = 320
MEMBERS = 16


def shard_levels(own_key, extent, shards, least, largest):
    factor_of = 1.0
    for axis_at, blocks in shards:
        steps = jax.random.uniform(jax.random.fold_in(jax.random.fold_in(own_key, 6), axis_at), (blocks,), jnp.float32, least / len(shards), largest / len(shards))
        factor_of = factor_of * jnp.repeat(jnp.exp(steps), extent[axis_at] // blocks).reshape((-1,) + (1,) * (len(extent) - 1 - axis_at))
    return factor_of


def gaussian(stream_key, shape, scale, reach, split=(), held_as=jnp.bfloat16):
    drawn = scale * jax.random.normal(stream_key, shape, jnp.float32)
    if split:
        drawn = drawn * shard_levels(stream_key, shape, split, -0.22, 0.18)
    return jnp.clip(drawn, -reach, reach).astype(held_as)


def setup_inputs(seed: int = 0) -> dict:
    keys = jax.random.split(jax.random.key(seed), 4)
    members = gaussian(keys[0], (MEMBERS, VARS, NLAT, NLON), 1.0, 6.0, ((0, 16), (2, 32)))
    analysis = gaussian(keys[1], (VARS, NLAT, NLON), 1.0, 6.0, ((1, 32),))
    wave_order = jax.random.permutation(keys[2], M).astype(jnp.int32)
    return dict(members=members, analysis=analysis, wave_order=wave_order)


SOFTNESS = 0.1
CEILING = 2.0 ** 60
SHRINK = 2.0 ** (-60)
LOG_SHIFT = 60.0 * math.log(2.0)
degree_block = 32

def fourier_table(wave_order, count_lon):
    lon_index = jnp.arange(count_lon, dtype=jnp.int32)
    product = lon_index[:, None] * wave_order[None, :].astype(jnp.int32) % count_lon
    angle = 2.0 * math.pi / count_lon * product.astype(jnp.float32)
    norm_lon = 1.0 / math.sqrt(count_lon)
    return jnp.stack([jnp.cos(angle) * norm_lon, -jnp.sin(angle) * norm_lon], axis=-1).astype(jnp.bfloat16)

def degree_step(carry, degree, wave_f, cosine, weight):
    previous, older, scale_prev, log_scale = carry
    denom = jnp.maximum(degree * degree - wave_f * wave_f, 1.0)
    factor = jnp.sqrt(jnp.maximum(4.0 * degree * degree - 1.0, 1.0) / denom)
    recurred = factor * (cosine * previous - older / scale_prev)
    current = jnp.where(degree < wave_f, 0.0, jnp.where(degree == wave_f, 1.0, recurred))
    too_large = jnp.abs(current) > CEILING
    current = jnp.where(too_large, current * SHRINK, current)
    previous = jnp.where(too_large, previous * SHRINK, previous)
    log_scale = jnp.where(too_large, log_scale + LOG_SHIFT, log_scale)
    carried = jnp.where(degree > wave_f, factor, 1.0)
    produced = (weight * (current * jnp.exp(log_scale))).astype(jnp.bfloat16)
    return ((current, previous, carried, log_scale), produced)

def legendre_rows(slot_waves, count_lat, count_degree):
    lat_index = jnp.arange(count_lat, dtype=jnp.int32).astype(jnp.float32)
    colatitude = (lat_index + 0.5) * (math.pi / count_lat)
    cosine = jnp.cos(colatitude)[None, :]
    sine_row = jnp.sin(colatitude)[None, :]
    weight = math.sqrt(math.pi / count_lat) * sine_row
    wave_f = slot_waves.astype(jnp.float32)[:, None]
    start_log = 0.5 * (lax.lgamma(wave_f + 1.5) - lax.lgamma(wave_f + 1.0) - lax.lgamma(jnp.float32(1.5)) + math.log(0.5)) + wave_f * jnp.log(sine_row)
    zero_rows = jnp.zeros((slot_waves.shape[0], count_lat), jnp.float32)
    initial = (zero_rows, zero_rows, jnp.ones((slot_waves.shape[0], 1), jnp.float32), start_log)

    def block_step(carry, first_degree):
        emitted = []
        for offset in range(degree_block):
            degree = (first_degree + offset).astype(jnp.float32)
            carry, produced = degree_step(carry, degree, wave_f, cosine, weight)
            emitted.append(produced)
        return (carry, jnp.stack(emitted))
    starts = jnp.arange(count_degree // degree_block, dtype=jnp.int32) * degree_block
    _, rows_out = lax.scan(block_step, initial, starts)
    return rows_out.reshape(count_degree, slot_waves.shape[0], count_lat)

def crps_terms(spectra):
    count_members = spectra.shape[0]
    smooth_abs = jnp.sqrt(spectra * spectra + SOFTNESS * SOFTNESS)
    pair_diff = spectra[:, None] - spectra[None, :]
    pair_abs = jnp.sqrt(pair_diff * pair_diff + SOFTNESS * SOFTNESS)
    coef_grad = spectra / smooth_abs - lax.optimization_barrier(jnp.sum(pair_diff / pair_abs, axis=1)) / (count_members - 1)
    per_coef = lax.optimization_barrier(jnp.sum(smooth_abs - SOFTNESS, axis=0)) / count_members - lax.optimization_barrier(jnp.sum(pair_abs - SOFTNESS, axis=(0, 1))) / (2 * count_members * (count_members - 1))
    return (coef_grad, lax.optimization_barrier(jnp.sum(per_coef, axis=(-2, -1))))

def reference(members, analysis, wave_order):
    count_members = members.shape[0]
    table_full = fourier_table(wave_order, NLON)
    table_wide = table_full.astype(jnp.float32)

    def forward(member):
        deviation = (member.astype(jnp.float32) - analysis.astype(jnp.float32)).astype(jnp.bfloat16)
        return jnp.einsum('vjk,ksp->sjpv', deviation.astype(jnp.float32), table_wide).astype(jnp.bfloat16)
    fourier = jnp.transpose(lax.map(forward, members), (1, 0, 2, 3, 4))
    groups = math.gcd(M, 32)
    width = M // groups

    def group_pass(group):
        start = (group * width).astype(jnp.int32)
        slot_waves = lax.dynamic_slice_in_dim(wave_order, start, width)
        legendre = legendre_rows(slot_waves, NLAT, L).astype(jnp.float32)
        fourier_part = lax.dynamic_slice_in_dim(fourier, start, width, 0).astype(jnp.float32)
        spectra = jnp.einsum('lsj,sejpv->selpv', legendre, fourier_part).astype(jnp.bfloat16)
        coef_grad, totals = lax.map(crps_terms, spectra.astype(jnp.float32))
        coef_grad = coef_grad.astype(jnp.bfloat16).astype(jnp.float32)
        returned = jnp.einsum('lsj,selpv->sejpv', legendre, coef_grad).astype(jnp.bfloat16)
        return (returned, totals / (2 * VARS))
    returned, totals = lax.map(group_pass, jnp.arange(groups, dtype=jnp.int32))
    returned = returned.reshape(M, count_members, NLAT, 2, VARS)
    returned = jnp.transpose(returned, (1, 0, 2, 3, 4))

    def inverse(block):
        return jnp.einsum('sjpv,ksp->vjk', block.astype(jnp.float32), table_wide).astype(jnp.bfloat16)
    grid_grad = lax.map(inverse, returned)
    return (grid_grad, totals.reshape(M, L))
```

```python
import math

import jax
import jax.numpy as jnp
import numpy as np
from jax import lax
from jax.experimental import pallas as pl
from jax.experimental.pallas import tpu as pltpu
from jax.sharding import PartitionSpec as P

SOFT2 = 0.1 * 0.1
CEILING = 2.0**60
SHRINK = 2.0 ** (-60)
LOG_SHIFT = 60.0 * math.log(2.0)
NLON, NLAT, DEG, MEM = 720, 384, 320, 16
GROUPS, VB = 5, 16
LANE = 128
MESH_AXES = ("ens", "lat")


def message_order():
    g, v, j = np.meshgrid(np.arange(GROUPS), np.arange(VB), np.arange(16), indexing="ij")
    extra = j - 8
    row = np.where(j < 8, j, 2 * extra + (g >= 3))
    lane = np.where(j < 8, 16 * g + v, 80 + 16 * (g - 3 * (g >= 3)) + v)
    place = np.where(j < 12, row * LANE + lane, -1).reshape(-1)
    return (place[:, None] == np.arange(8 * LANE)[None, :]).astype(jnp.bfloat16)


def latitude_order():
    row = np.arange(256)
    jb, c = row // 8, row % 8
    return np.concatenate([12 * jb + c, 12 * jb + 8 + c // 2])


def dot(a, b, dims=((1,), (0,))):
    return lax.dot_general(a, b, (dims, ((), ())), preferred_element_type=jnp.float32)


SIN_TERMS = [(-1) ** n / math.factorial(2 * n + 1) for n in range(7)]


def fourier_block(wave, part):
    lon = lax.broadcasted_iota(jnp.int32, (32, NLON), 1).astype(jnp.float32)
    turn = wave * lon + 180.0 * part
    turn = turn - NLON * jnp.floor((turn + 0.5) * (1.0 / NLON))
    x = (jnp.abs(turn - 360.0) - 180.0) * (math.pi / 360.0)
    x2 = x * x
    total = SIN_TERMS[6]
    for term in SIN_TERMS[5::-1]:
        total = total * x2 + term
    return total * x * (1.0 / math.sqrt(NLON))


def forward_kernel(wave_ref, order_ref, members_ref, analysis_ref, sent_ref, table_ref, dev, rows):
    @pl.when(pl.program_id(0) == 0)
    def _():
        dev[...] = jnp.zeros_like(dev)
        for g in range(GROUPS):
            for sb in range(4):
                pair = 5 * sb + g
                wave = wave_ref[:, pair // 2 : pair // 2 + 1]
                at = g * LANE + sb * 32
                table_ref[at : at + 32, :] = fourier_block(wave, pair % 2).astype(jnp.bfloat16)

    dev[:, 0:12, :] = members_ref[0].astype(jnp.float32) - analysis_ref[...].astype(jnp.float32)
    deviation = dev[...].reshape(256, NLON).astype(jnp.bfloat16)
    fourier = dot(table_ref[...], deviation, ((1,), (1,))).astype(jnp.bfloat16)
    wide = jnp.concatenate([fourier[g * LANE : (g + 1) * LANE] for g in range(GROUPS)], axis=1)
    placed = dot(wide, order_ref[...])
    for c in range(8):
        rows[pl.ds(c, LANE, stride=8), :] = placed[:, c * LANE : (c + 1) * LANE]
    sent_ref[...] = rows[...].reshape(LANE, 8, LANE).astype(jnp.bfloat16)


def legendre_kernel(wave_ref, base_ref, cos_ref, logsin_ref, weight_ref, leg_ref, legt_ref, rows):
    wave = jnp.broadcast_to(wave_ref[...], (8, 512))
    wave2 = wave * wave
    cosine = jnp.broadcast_to(cos_ref[...], (8, 512))
    weight = jnp.broadcast_to(weight_ref[...], (8, 512))
    start_log = base_ref[...] + wave * logsin_ref[...]
    zero = jnp.zeros((8, 512), jnp.float32)

    def block(b, carry):
        for offset in range(8):
            previous, older, inverse, log_scale = carry
            index = b * 8 + offset
            degree = index.astype(jnp.float32)
            square = jnp.full((8, 512), degree * degree, jnp.float32)
            ratio = jnp.maximum(square - wave2, 1.0) / jnp.maximum(4.0 * square - 1.0, 1.0)
            factor = lax.rsqrt(ratio)
            current = factor * (cosine * previous - older * inverse)
            current = jnp.where(wave == degree, 1.0, current)
            too_large = jnp.abs(current) > CEILING
            shrink = jnp.where(too_large, SHRINK, 1.0)
            log_scale = jnp.where(too_large, log_scale + LOG_SHIFT, log_scale)
            current = current * shrink
            previous = previous * shrink
            value = weight * (current * jnp.exp(log_scale))
            for q in range(4):
                rows[q, pl.ds(pl.multiple_of(index * 8, 8), 8), :] = value[:, q * LANE : (q + 1) * LANE]
            carry = (current, previous, ratio * factor, log_scale)
        return carry

    lax.fori_loop(0, DEG // 8, block, (zero, zero, zero + 1.0, start_log))
    for s in range(3):
        for q in range(4):
            part = rows[q, pl.ds(s, DEG, stride=8), :]
            at = s * 512 + q * LANE
            leg_ref[:, at : at + LANE] = part.astype(jnp.bfloat16)
            padded = jnp.concatenate([part, jnp.zeros((64, LANE), jnp.float32)], axis=0)
            legt_ref[q * LANE : (q + 1) * LANE, s * DEG : (s + 1) * DEG] = padded.T[:, :DEG].astype(
                jnp.bfloat16
            )


def score_kernel(got_ref, leg_ref, legt_ref, sent_ref, coef, per):
    own_lat = lax.axis_index("lat")
    odd_block = lax.rem(lax.axis_index("ens"), 2)
    lane = lax.broadcasted_iota(jnp.int32, (256, LANE), 1)
    even_row = lax.rem(lax.broadcasted_iota(jnp.int32, (256, LANE), 0), 2) == 0
    slot_of = jnp.where(lane < 80, (lane // 16 + odd_block) // 2, -1)
    extra_slot = jnp.where(even_row == (lane < 48), slot_of, -1)

    def spectra_pair(pair, _):
        halves = []
        for k in range(2):
            first = pl.multiple_of((2 * pair + k) * 32, 32)
            main = got_ref[pl.ds(first, 32)].astype(jnp.float32).reshape(256, LANE)
            extra = jnp.where(even_row, pltpu.roll(main, 48, 1), pltpu.roll(main, 96, 1))
            stack = []
            for s in range(3):
                stack.append(jnp.where(slot_of == s, main, 0.0).astype(jnp.bfloat16))
                stack.append(jnp.where(extra_slot == s, extra, 0.0).astype(jnp.bfloat16))
            halves.append(jnp.concatenate(stack, axis=0))
        spectra = dot(leg_ref[...], jnp.concatenate(halves, axis=1))
        spectra = spectra.astype(jnp.bfloat16).astype(jnp.float32)
        for k in range(2):
            coef[2 * pair + k] = spectra[:, k * LANE : (k + 1) * LANE]
        return 0

    lax.fori_loop(0, MEM // 2, spectra_pair, 0)

    def degrees(tile, _):
        at = pl.ds(pl.multiple_of(tile * 8, 8), 8)
        z = [coef[e, at, :] for e in range(MEM)]
        pull = [None] * MEM
        inverse_sum = None
        for a in range(MEM):
            for b in range(a + 1, MEM):
                diff = z[a] - z[b]
                inverse = lax.rsqrt(diff * diff + SOFT2)
                term = diff * inverse
                inverse_sum = inverse if inverse_sum is None else inverse_sum + inverse
                pull[a] = term if pull[a] is None else pull[a] + term
                pull[b] = -term if pull[b] is None else pull[b] - term
        pair_abs = SOFT2 * inverse_sum
        single = None
        for e in range(MEM):
            square = z[e] * z[e] + SOFT2
            inverse = lax.rsqrt(square)
            soft = square * inverse
            single = soft if single is None else single + soft
            pair_abs = pair_abs + z[e] * pull[e]
            coef[e, at, :] = z[e] * inverse - pull[e] * (1.0 / (MEM - 1))
        per[at, :] = (single - 0.1 * MEM) * (1.0 / MEM) - (pair_abs - 0.1 * (MEM * (MEM - 1) // 2)) * (
            1.0 / (MEM * (MEM - 1))
        )
        return 0

    lax.fori_loop(0, DEG // 8, degrees, 0)

    row = lax.broadcasted_iota(jnp.int32, (LANE, LANE), 0)
    col = lax.broadcasted_iota(jnp.int32, (LANE, LANE), 1) - 112
    row_slot = jnp.where(row < 80, (row // 16 + odd_block) // 2, -1)
    col_slot = jnp.where((col >= 0) & (col < 15), (col + 25) // 5 - 5, -2)
    gather = jnp.where(row_slot == col_slot, 1.0, 0.0)
    summed = lax.dot_general(
        per[...],
        gather,
        (((1,), (0,)), ((), ())),
        precision=lax.Precision.HIGHEST,
        preferred_element_type=jnp.float32,
    )
    degree = lax.broadcasted_iota(jnp.int32, (DEG, LANE), 0)
    column = lax.broadcasted_iota(jnp.int32, (DEG, LANE), 1) - 110
    keep = (column >= 2) & (lax.rem(degree, 5) == lax.rem(column + 3, 5))
    summed = jnp.where(keep, summed, 0.0).astype(jnp.bfloat16)
    out_row = lax.broadcasted_iota(jnp.int32, (LANE, DEG), 0)
    out_deg = lax.broadcasted_iota(jnp.int32, (LANE, DEG), 1)
    want = (out_row // 8) * 4 + lax.rem(out_row, 8) // 2
    pick = (lax.rem(out_row, 2) == 1) & (out_deg // 5 == want)
    scores = dot(jnp.where(pick, 1.0, 0.0).astype(jnp.bfloat16), summed)
    per[0:LANE, :] = scores

    def returned_pair(pair, _):
        halves = []
        for k in range(2):
            grad = coef[2 * pair + k]
            halves.append(
                jnp.concatenate(
                    [jnp.where(slot_of[0:1] == s, grad, 0.0).astype(jnp.bfloat16) for s in range(3)], axis=0
                )
            )
        back = dot(legt_ref[...], jnp.concatenate(halves, axis=1))
        for k in range(2):
            main = back[0:256, k * LANE : (k + 1) * LANE]
            extra = back[256:512, k * LANE : (k + 1) * LANE]
            extra = jnp.where(even_row, pltpu.roll(extra, 80, 1), pltpu.roll(extra, 32, 1))
            message = jnp.where(lane < 80, main, extra).reshape(32, 8, LANE)
            member = 2 * pair + k
            own = lax.broadcasted_iota(jnp.int32, (32, 8, LANE), 0) == own_lat
            score = per[pl.ds(pl.multiple_of(member * 8, 8), 8), :][None]
            message = jnp.where(own, message + score, message)
            sent_ref[pl.ds(pl.multiple_of(member * 32, 32), 32)] = message.astype(jnp.bfloat16)
        return 0

    lax.fori_loop(0, MEM // 2, returned_pair, 0)


def inverse_kernel(got_ref, order_ref, table_ref, grid_ref, score_ref, rows):
    own_lat = lax.axis_index("lat")
    step = pl.program_id(0)
    rows[...] = got_ref[...].astype(jnp.float32).reshape(256 * 8, LANE)
    got = jnp.concatenate([rows[pl.ds(c, 256, stride=8), :] for c in range(8)], axis=1).astype(jnp.bfloat16)
    turned = dot(order_ref[...], got, ((1,), (1,))).astype(jnp.bfloat16)
    for half in range(2):
        left = jnp.concatenate(
            [turned[g * 256 : (g + 1) * 256, half * LANE : (half + 1) * LANE] for g in range(GROUPS)], axis=1
        )
        grid = dot(left, table_ref[...]).reshape(16, 16, NLON)[:, 0:12, :]
        grid_ref[0, half * 16 : (half + 1) * 16] = grid.astype(jnp.bfloat16)
    for sb in range(4):
        part = None
        for half in range(2):
            at = pl.multiple_of((half * LANE + sb * 32 + own_lat) * 8, 8)
            tile = rows[pl.ds(at, 8), :]
            part = tile if part is None else part + tile
        score_ref[sb] = jnp.where(step == 0, part, score_ref[sb] + part)


def body(members, analysis, wave_order):
    order = jnp.asarray(message_order())
    block_mib = 1 << 20
    waves = wave_order.astype(jnp.float32)
    sent, table = pl.pallas_call(
        forward_kernel,
        grid=(4,),
        in_specs=[
            pl.BlockSpec((32, 10), lambda i: (0, 0)),
            pl.BlockSpec((1280, 1024), lambda i: (0, 0)),
            pl.BlockSpec((1, 16, 12, NLON), lambda i: (0, i, 0, 0)),
            pl.BlockSpec((16, 12, NLON), lambda i: (i, 0, 0)),
        ],
        out_specs=[
            pl.BlockSpec((LANE, 8, LANE), lambda i: (i, 0, 0)),
            pl.BlockSpec((640, NLON), lambda i: (0, 0)),
        ],
        out_shape=[
            jax.ShapeDtypeStruct((512, 8, LANE), jnp.bfloat16),
            jax.ShapeDtypeStruct((640, NLON), jnp.bfloat16),
        ],
        scratch_shapes=[pltpu.VMEM((16, 16, NLON), jnp.float32), pltpu.VMEM((1024, LANE), jnp.float32)],
        compiler_params=pltpu.CompilerParams(vmem_limit_bytes=32 * block_mib),
        cost_estimate=pl.CostEstimate(flops=3 * 10**9, bytes_accessed=8 * 10**6, transcendentals=0),
        name="forward",
    )(waves.reshape(32, 10), order, members, analysis)
    got = lax.all_to_all(sent, MESH_AXES, 0, 0, tiled=True)

    own = lax.axis_index("lat") * 10 + (5 * lax.rem(lax.axis_index("ens"), 4)) // 2
    slots = lax.dynamic_slice_in_dim(waves, own, 3)
    slots = jnp.concatenate([slots, jnp.broadcast_to(slots[2:3], (5,))]).reshape(8, 1)
    base = 0.5 * (
        lax.lgamma(slots + 1.5) - lax.lgamma(slots + 1.0) - lax.lgamma(jnp.float32(1.5)) + math.log(0.5)
    )
    colatitude = (latitude_order() + 0.5) * (math.pi / NLAT)
    constants = [np.cos(colatitude), np.log(np.sin(colatitude)), math.sqrt(math.pi / NLAT) * np.sin(colatitude)]
    constants = [jnp.asarray(c[None].astype(np.float32)) for c in constants]
    legendre, legendre_t = pl.pallas_call(
        legendre_kernel,
        out_shape=[
            jax.ShapeDtypeStruct((DEG, 1536), jnp.bfloat16),
            jax.ShapeDtypeStruct((512, 960), jnp.bfloat16),
        ],
        scratch_shapes=[pltpu.VMEM((4, DEG * 8, LANE), jnp.float32)],
        compiler_params=pltpu.CompilerParams(vmem_limit_bytes=32 * block_mib),
        cost_estimate=pl.CostEstimate(flops=10**8, bytes_accessed=2 * 10**6, transcendentals=3 * 10**6),
        name="legendre",
    )(slots, base, *constants)

    sent = pl.pallas_call(
        score_kernel,
        out_shape=jax.ShapeDtypeStruct((512, 8, LANE), jnp.bfloat16),
        scratch_shapes=[pltpu.VMEM((MEM, DEG, LANE), jnp.float32), pltpu.VMEM((DEG, LANE), jnp.float32)],
        compiler_params=pltpu.CompilerParams(vmem_limit_bytes=40 * block_mib),
        cost_estimate=pl.CostEstimate(flops=6 * 10**9, bytes_accessed=5 * 10**6, transcendentals=5 * 10**6),
        name="score",
    )(got, legendre, legendre_t)
    got = lax.all_to_all(sent, MESH_AXES, 0, 0, tiled=True)

    grid_grad, parts = pl.pallas_call(
        inverse_kernel,
        grid=(2,),
        in_specs=[
            pl.BlockSpec((256, 8, LANE), lambda i: (i, 0, 0)),
            pl.BlockSpec((1280, 1024), lambda i: (0, 0)),
            pl.BlockSpec((640, NLON), lambda i: (0, 0)),
        ],
        out_specs=[
            pl.BlockSpec((1, 32, 12, NLON), lambda i: (0, i, 0, 0)),
            pl.BlockSpec((4, 8, LANE), lambda i: (0, 0, 0)),
        ],
        out_shape=[
            jax.ShapeDtypeStruct((1, 64, 12, NLON), jnp.bfloat16),
            jax.ShapeDtypeStruct((4, 8, LANE), jnp.float32),
        ],
        scratch_shapes=[pltpu.VMEM((2048, LANE), jnp.float32)],
        compiler_params=pltpu.CompilerParams(vmem_limit_bytes=40 * block_mib),
        cost_estimate=pl.CostEstimate(flops=3 * 10**9, bytes_accessed=8 * 10**6, transcendentals=0),
        name="inverse",
    )(got, order, table)
    parts = parts[:, 1::2, 112:127].reshape(4, 4, 3, 5).transpose(0, 2, 1, 3).reshape(4, 3, 20) / (2 * 64)
    halves = [
        jnp.concatenate([parts[k, :2], parts[k, 2:] + parts[k + 1, :1], parts[k + 1, 1:]]) for k in (0, 2)
    ]
    return (grid_grad, jnp.concatenate(halves))


def solution(mesh):
    placed = (P("ens", None, "lat", None), P(None, "lat", None), P())
    return jax.shard_map(
        body,
        mesh=mesh,
        in_specs=placed,
        out_specs=(P("ens", None, "lat", None), P("lat", "ens")),
        check_vma=False,
    )
```

```python
import math

import jax
import jax.numpy as jnp
import numpy as np
from jax import lax
from jax.experimental import pallas as pl
from jax.experimental.pallas import tpu as pltpu
from jax.sharding import PartitionSpec as P

SOFT2 = 0.1 * 0.1
CEILING = 2.0**60
SHRINK = 2.0 ** (-60)
LOG_SHIFT = 60.0 * math.log(2.0)
NLON, NLAT, DEG, MEM = 720, 384, 320, 16
GROUPS, VB = 5, 16
LANE = 128
MESH_AXES = ("ens", "lat")


def message_order(rows, width):
    shape = (GROUPS * rows, width)
    row = lax.broadcasted_iota(jnp.int32, shape, 0)
    lane = lax.broadcasted_iota(jnp.int32, shape, 1)
    g, inner = row // rows, row % rows
    k, v = inner % 64 // VB, row % VB
    second = jnp.where(g >= 3, 1, 0)
    plain = k * LANE + 16 * g + v
    extra = second * LANE + 80 + 16 * (g - 3 * second) + v
    place = jnp.where(k < 2, plain, jnp.where(k == 2, extra, -1024))
    place = place + 256 * (inner // 64)
    return jnp.where(place == lane, 1.0, 0.0).astype(jnp.bfloat16)


def latitude_order():
    row = np.arange(256)
    jb, c = row // 8, row % 8
    return np.concatenate([12 * jb + c, 12 * jb + 8 + c // 2])


def dot(a, b, dims=((1,), (0,))):
    return lax.dot_general(a, b, (dims, ((), ())), preferred_element_type=jnp.float32)


SIN_TERMS = [(-1) ** n / math.factorial(2 * n + 1) for n in range(7)]


def fourier_block(wave, part):
    lon = lax.broadcasted_iota(jnp.int32, (32, NLON), 1).astype(jnp.float32)
    turn = wave * lon + 180.0 * part
    turn = turn - NLON * jnp.floor((turn + 0.5) * (1.0 / NLON))
    x = (jnp.abs(turn - 360.0) - 180.0) * (math.pi / 360.0)
    x2 = x * x
    total = SIN_TERMS[6]
    for term in SIN_TERMS[5::-1]:
        total = total * x2 + term
    return total * x * (1.0 / math.sqrt(NLON))


def forward_kernel(wave_ref, members_hbm, analysis_hbm, sent_ref, table_ref, members, analysis, rows, sems):
    loads = [
        pltpu.make_async_copy(members_hbm, members, sems.at[0]),
        pltpu.make_async_copy(analysis_hbm, analysis, sems.at[1]),
    ]
    for load in loads:
        load.start()
    waves = jnp.broadcast_to(wave_ref[...].reshape(1, DEG).astype(jnp.float32), (32, DEG))
    ahead = lax.broadcasted_iota(jnp.int32, (32, DEG), 1) - 10 * lax.broadcasted_iota(jnp.int32, (32, DEG), 0)
    columns = [jnp.sum(jnp.where(ahead == k, waves, 0.0), axis=1, keepdims=True) for k in range(10)]
    for g in range(GROUPS):
        for sb in range(4):
            pair = 5 * sb + g
            at = g * LANE + sb * 32
            table_ref[at : at + 32, :] = fourier_block(columns[pair // 2], pair % 2).astype(jnp.bfloat16)
    order = message_order(LANE, 512)
    for load in loads:
        load.wait()

    deviation = (members[0].astype(jnp.float32) - analysis[...].astype(jnp.float32)).astype(jnp.bfloat16)
    blank = jnp.zeros((VB, NLON), jnp.bfloat16)
    for h in range(2):
        pieces = []
        for t in range(4):
            for vb in (2 * h, 2 * h + 1):
                pieces += [deviation[j, vb * VB : (vb + 1) * VB] for j in (2 * t, 2 * t + 1, 8 + t)] + [blank]
        fourier = dot(table_ref[...], jnp.concatenate(pieces, axis=0), ((1,), (1,))).astype(jnp.bfloat16)
        wide = jnp.concatenate(
            [
                jnp.concatenate(
                    [fourier[g * LANE : (g + 1) * LANE, t * LANE : (t + 1) * LANE] for g in range(GROUPS)],
                    axis=1,
                )
                for t in range(4)
            ],
            axis=0,
        )
        placed = dot(wide, order)
        for t in range(4):
            for q in range(4):
                at = (q // 2) * LANE * 8 + 2 * t + q % 2
                rows[pl.ds(at, LANE, stride=8), :] = placed[
                    t * LANE : (t + 1) * LANE, q * LANE : (q + 1) * LANE
                ]
        sent_ref[h * 256 : (h + 1) * 256] = rows[...].reshape(256, 8, LANE).astype(jnp.bfloat16)


def legendre_kernel(wave_ref, base_ref, cos_ref, logsin_ref, weight_ref, leg_ref, rows):
    wave = jnp.broadcast_to(wave_ref[...], (8, 512))
    wave2 = wave * wave
    cosine = jnp.broadcast_to(cos_ref[...], (8, 512))
    weight = jnp.broadcast_to(weight_ref[...], (8, 512))
    start_log = base_ref[...] + wave * logsin_ref[...]
    zero = jnp.zeros((8, 512), jnp.float32)

    def block(b, carry):
        for offset in range(8):
            previous, older, inverse, log_scale = carry
            index = b * 8 + offset
            degree = index.astype(jnp.float32)
            square = jnp.full((8, 512), degree * degree, jnp.float32)
            ratio = jnp.maximum(square - wave2, 1.0) / jnp.maximum(4.0 * square - 1.0, 1.0)
            factor = lax.rsqrt(ratio)
            current = factor * (cosine * previous - older * inverse)
            current = jnp.where(wave == degree, 1.0, current)
            too_large = jnp.abs(current) > CEILING
            shrink = jnp.where(too_large, SHRINK, 1.0)
            log_scale = jnp.where(too_large, log_scale + LOG_SHIFT, log_scale)
            current = current * shrink
            previous = previous * shrink
            value = weight * (current * jnp.exp(log_scale))
            for q in range(4):
                rows[q, pl.ds(pl.multiple_of(index * 8, 8), 8), :] = value[:, q * LANE : (q + 1) * LANE]
            carry = (current, previous, ratio * factor, log_scale)
        return carry

    lax.fori_loop(0, DEG // 8, block, (zero, zero, zero + 1.0, start_log))
    for s in range(3):
        for q in range(4):
            part = rows[q, pl.ds(s, DEG, stride=8), :]
            at = s * 512 + q * LANE
            leg_ref[:, at : at + LANE] = part.astype(jnp.bfloat16)


def pair_terms(z):
    pull = [None] * MEM
    inverse_sum = None
    for a in range(MEM):
        for b in range(a + 1, MEM):
            diff = z[a] - z[b]
            inverse = lax.rsqrt(diff * diff + SOFT2)
            term = diff * inverse
            inverse_sum = inverse if inverse_sum is None else inverse_sum + inverse
            pull[a] = term if pull[a] is None else pull[a] + term
            pull[b] = -term if pull[b] is None else pull[b] - term
    pair_abs = SOFT2 * inverse_sum
    single = None
    grads = []
    for e in range(MEM):
        square = z[e] * z[e] + SOFT2
        inverse = lax.rsqrt(square)
        soft = square * inverse
        single = soft if single is None else single + soft
        pair_abs = pair_abs + z[e] * pull[e]
        grads.append(z[e] * inverse - pull[e] * (1.0 / (MEM - 1)))
    pairs = MEM * (MEM - 1)
    return grads, (single - 0.1 * MEM) * (1.0 / MEM) - (pair_abs - 0.1 * (pairs // 2)) * (1.0 / pairs)


def score_kernel(got_ref, leg_ref, sent_ref, turned, coef, sums, scores):
    own_lat = lax.axis_index("lat")
    odd_block = lax.rem(lax.axis_index("ens"), 2)
    even = lax.rem(lax.broadcasted_iota(jnp.int32, (48, 256), 1), 2) == 0
    unit = lax.broadcasted_iota(jnp.int32, (256, 256), 0) == lax.broadcasted_iota(jnp.int32, (256, 256), 1)
    unit = jnp.where(unit, 1.0, 0.0).astype(jnp.bfloat16)

    def slot_lanes(g):
        return pl.ds(pl.multiple_of((g + odd_block) // 2 * 512, 512), 512)

    def turn(member, _):
        message = got_ref[pl.ds(pl.multiple_of(member * 32, 32), 32)].astype(jnp.float32)
        message = message.reshape(256, LANE).astype(jnp.bfloat16)
        rows = dot(unit[:LANE, :LANE], message, ((1,), (1,)))
        at = pl.ds(pl.multiple_of(member * VB, VB), VB)
        low = jnp.where(even, rows[80:128], 0.0).astype(jnp.bfloat16)
        high = jnp.where(even, 0.0, rows[80:128]).astype(jnp.bfloat16)
        for g in range(GROUPS):
            turned[g, at, 0:256] = rows[g * VB : (g + 1) * VB].astype(jnp.bfloat16)
            extra = low[g * VB : (g + 1) * VB] if g < 3 else high[(g - 3) * VB : (g - 2) * VB]
            turned[g, at, 256:512] = extra
        return 0

    lax.fori_loop(0, MEM, turn, 0, unroll=4)

    first_half = lax.broadcasted_iota(jnp.int32, (8, LANE), 1) < 64

    def group(g, _):
        spectra = dot(turned[g], leg_ref[:, slot_lanes(g)], ((1,), (1,)))
        coef[:, 0:DEG] = spectra.astype(jnp.bfloat16).astype(jnp.float32)
        for q in range(2):
            lanes = slice(q * LANE, (q + 1) * LANE)
            total = None
            for r in range(2):
                grads, per = pair_terms([coef[e * VB + r * 8 : e * VB + r * 8 + 8, lanes] for e in range(MEM)])
                for e in range(MEM):
                    coef[e * VB + r * 8 : e * VB + r * 8 + 8, lanes] = grads[e]
                total = per if total is None else total + per
            sums[g, :, lanes] = total
        lanes = slice(2 * LANE, 3 * LANE)
        packed = []
        for e in range(MEM):
            top, bottom = coef[e * VB : e * VB + 8, lanes], coef[e * VB + 8 : e * VB + VB, lanes]
            packed.append(jnp.where(first_half, top, pltpu.roll(bottom, 64, 1)))
        grads, per = pair_terms(packed)
        for e in range(MEM):
            coef[e * VB : e * VB + 8, lanes] = grads[e]
            coef[e * VB + 8 : e * VB + VB, lanes] = pltpu.roll(grads[e], 64, 1)
        sums[g, :, lanes] = per + pltpu.roll(per, 64, 1)
        grad = coef[:, 0:DEG].astype(jnp.bfloat16)
        turned[g] = dot(grad, leg_ref[:, slot_lanes(g)]).astype(jnp.bfloat16)
        return 0

    lax.fori_loop(0, GROUPS, group, 0)

    place = lax.broadcasted_iota(jnp.int32, (16, DEG), 0)
    same = lax.rem(lax.broadcasted_iota(jnp.int32, (16, DEG), 1), 5) == lax.rem(place, 5)
    spread = jnp.zeros((16, DEG), jnp.float32)
    for g in range(GROUPS):
        mine = same & (place < 15) & (place // 5 == (g + odd_block) // 2)
        score = jnp.sum(sums[g], axis=0, keepdims=True)[:, 0:DEG]
        spread = spread + jnp.where(mine, jnp.broadcast_to(score, (16, DEG)), 0.0)
    spread = jnp.concatenate([jnp.zeros((112, DEG), jnp.float32), spread], axis=0).astype(jnp.bfloat16)
    out_row = lax.broadcasted_iota(jnp.int32, (LANE, DEG), 0)
    out_deg = lax.broadcasted_iota(jnp.int32, (LANE, DEG), 1)
    pick = (lax.rem(out_row, 2) == 1) & (out_deg // 5 == (out_row // 8) * 4 + lax.rem(out_row, 8) // 2)
    scores[...] = dot(jnp.where(pick, 1.0, 0.0).astype(jnp.bfloat16), spread, ((1,), (1,)))

    def send(pair, _):
        rows = []
        for k in range(2):
            at = pl.ds(pl.multiple_of((2 * pair + k) * VB, VB), VB)
            rows += [turned[g, at, 0:256] for g in range(GROUPS)]
            extra = [turned[g, at, 256:512].astype(jnp.float32) for g in range(GROUPS)]
            blank = jnp.zeros((VB, 256), jnp.float32)
            extra = jnp.where(even, jnp.concatenate(extra[:3]), jnp.concatenate(extra[3:] + [blank]))
            rows.append(extra.astype(jnp.bfloat16))
        back = dot(unit, jnp.concatenate(rows, axis=0), ((1,), (1,)))
        for k in range(2):
            member = 2 * pair + k
            message = back[:, k * LANE : (k + 1) * LANE].reshape(32, 8, LANE)
            sent_ref[pl.ds(pl.multiple_of(member * 32, 32), 32)] = message.astype(jnp.bfloat16)
            score = scores[pl.ds(pl.multiple_of(member * 8, 8), 8), :]
            own = member * 32 + own_lat
            sent_ref[own] = (sent_ref[own].astype(jnp.float32) + score).astype(jnp.bfloat16)
        return 0

    lax.fori_loop(0, MEM // 2, send, 0, unroll=2)


def inverse_kernel(got_ref, table_ref, grid_hbm, score_ref, rows, grid, sems):
    own_lat = lax.axis_index("lat")
    order = message_order(64, 256)
    order = jnp.concatenate([order[g * 64 : g * 64 + 48] for g in range(GROUPS)], axis=0)
    rows[...] = got_ref[...].astype(jnp.float32).reshape(512 * 8, LANE)
    turned = []
    for t in range(4):
        pair = [rows[pl.ds(2 * t + c, 512, stride=8), :].astype(jnp.bfloat16) for c in range(2)]
        turned.append(dot(order, jnp.concatenate(pair, axis=1), ((1,), (1,))).astype(jnp.bfloat16))
    stores = []
    for h in range(2):
        left = []
        for vb in (2 * h, 2 * h + 1):
            for t in range(4):
                left.append(
                    jnp.concatenate(
                        [turned[t][g * 48 : (g + 1) * 48, vb * LANE : (vb + 1) * LANE] for g in range(GROUPS)],
                        axis=1,
                    )
                )
        result = dot(jnp.concatenate(left, axis=0), table_ref[...]).astype(jnp.bfloat16)
        for vb in range(2):
            for t in range(4):
                for k, j in enumerate((2 * t, 2 * t + 1, 8 + t)):
                    at = (vb * 4 + t) * 48 + k * VB
                    grid[0, j, h * 32 + vb * VB : h * 32 + (vb + 1) * VB, :] = result[at : at + VB]
        half = (slice(None), slice(None), slice(h * 32, (h + 1) * 32), slice(None))
        stores.append(pltpu.make_async_copy(grid.at[half], grid_hbm.at[half], sems.at[h]))
        stores[-1].start()

    slot = lax.broadcasted_iota(jnp.int32, (16, LANE), 0)
    column = lax.broadcasted_iota(jnp.int32, (16, LANE), 1) - 112
    parts = [None] * 4
    for sb in range(4):
        tile = None
        for vb in range(4):
            piece = rows[pl.ds(pl.multiple_of((vb * LANE + sb * 32 + own_lat) * 8, 8), 8), :]
            tile = piece if tile is None else tile + piece
        here = (column >= 0) & (slot == (5 * sb) // 2 + (column + 5) // 5 - 1)
        for t in range(4):
            spread = jnp.where(here, jnp.broadcast_to(tile[2 * t + 1 : 2 * t + 2], (16, LANE)), 0.0)
            parts[t] = spread if parts[t] is None else parts[t] + spread
    source = lax.broadcasted_iota(jnp.int32, (512, LANE), 0)
    target = lax.broadcasted_iota(jnp.int32, (512, LANE), 1)
    inside = source % LANE - 110
    fits = (inside >= 2) & (inside < 17) & (target == 5 * (source // LANE) + (inside + 3) % 5)
    scores = lax.dot_general(
        jnp.concatenate(parts, axis=1),
        jnp.where(fits, 1.0, 0.0),
        (((1,), (0,)), ((), ())),
        precision=lax.Precision.HIGHEST,
        preferred_element_type=jnp.float32,
    )
    score_ref[...] = scores[:10, :20] * (1.0 / 128)
    for store in stores:
        store.wait()


def body(members, analysis, wave_order):
    mib = 1 << 20
    any_spec = pl.BlockSpec(memory_space=pltpu.HBM)
    vmem_spec = pl.BlockSpec(memory_space=pltpu.VMEM)
    waves = wave_order.astype(jnp.float32)
    sent, table = pl.pallas_call(
        forward_kernel,
        in_specs=[vmem_spec, any_spec, any_spec],
        out_shape=[
            jax.ShapeDtypeStruct((512, 8, LANE), jnp.bfloat16),
            jax.ShapeDtypeStruct((640, NLON), jnp.bfloat16),
        ],
        scratch_shapes=[
            pltpu.VMEM((1, 12, 64, NLON), jnp.bfloat16),
            pltpu.VMEM((12, 64, NLON), jnp.bfloat16),
            pltpu.VMEM((2048, LANE), jnp.float32),
            pltpu.SemaphoreType.DMA((2,)),
        ],
        compiler_params=pltpu.CompilerParams(vmem_limit_bytes=60 * mib),
        cost_estimate=pl.CostEstimate(flops=3 * 10**9, bytes_accessed=4 * 10**6, transcendentals=0),
        name="forward",
    )(wave_order, members.transpose(0, 2, 1, 3), analysis.transpose(1, 0, 2))
    got = lax.all_to_all(sent, MESH_AXES, 0, 0, tiled=True)

    own = lax.axis_index("lat") * 10 + (5 * lax.rem(lax.axis_index("ens"), 4)) // 2
    slots = lax.dynamic_slice_in_dim(waves, own, 3)
    slots = jnp.concatenate([slots, jnp.broadcast_to(slots[2:3], (5,))]).reshape(8, 1)
    base = 0.5 * (
        lax.lgamma(slots + 1.5) - lax.lgamma(slots + 1.0) - lax.lgamma(jnp.float32(1.5)) + math.log(0.5)
    )
    colatitude = (latitude_order() + 0.5) * (math.pi / NLAT)
    constants = [np.cos(colatitude), np.log(np.sin(colatitude)), math.sqrt(math.pi / NLAT) * np.sin(colatitude)]
    constants = [jnp.asarray(c[None].astype(np.float32)) for c in constants]
    legendre = pl.pallas_call(
        legendre_kernel,
        out_shape=jax.ShapeDtypeStruct((DEG, 1536), jnp.bfloat16),
        scratch_shapes=[pltpu.VMEM((4, DEG * 8, LANE), jnp.float32)],
        compiler_params=pltpu.CompilerParams(vmem_limit_bytes=16 * mib),
        cost_estimate=pl.CostEstimate(flops=10**8, bytes_accessed=2 * 10**6, transcendentals=3 * 10**6),
        name="legendre",
    )(slots, base, *constants)

    sent = pl.pallas_call(
        score_kernel,
        out_shape=jax.ShapeDtypeStruct((512, 8, LANE), jnp.bfloat16),
        scratch_shapes=[
            pltpu.VMEM((GROUPS, MEM * VB, 512), jnp.bfloat16),
            pltpu.VMEM((MEM * VB, 3 * LANE), jnp.float32),
            pltpu.VMEM((GROUPS, 8, 3 * LANE), jnp.float32),
            pltpu.VMEM((LANE, LANE), jnp.float32),
        ],
        compiler_params=pltpu.CompilerParams(vmem_limit_bytes=20 * mib),
        cost_estimate=pl.CostEstimate(flops=6 * 10**9, bytes_accessed=5 * 10**6, transcendentals=5 * 10**6),
        name="score",
    )(got, legendre)
    got = lax.all_to_all(sent, MESH_AXES, 0, 0, tiled=True)

    grid_grad, coef_score = pl.pallas_call(
        inverse_kernel,
        in_specs=[vmem_spec, vmem_spec],
        out_specs=[any_spec, vmem_spec],
        out_shape=[
            jax.ShapeDtypeStruct((1, 12, 64, NLON), jnp.bfloat16),
            jax.ShapeDtypeStruct((10, 20), jnp.float32),
        ],
        scratch_shapes=[
            pltpu.VMEM((4096, LANE), jnp.float32),
            pltpu.VMEM((1, 12, 64, NLON), jnp.bfloat16),
            pltpu.SemaphoreType.DMA((2,)),
        ],
        compiler_params=pltpu.CompilerParams(vmem_limit_bytes=24 * mib),
        cost_estimate=pl.CostEstimate(flops=2 * 10**9, bytes_accessed=4 * 10**6, transcendentals=0),
        name="inverse",
    )(got, table)
    return (grid_grad.transpose(0, 2, 1, 3), coef_score)


def solution(mesh):
    placed = (P("ens", None, "lat", None), P(None, "lat", None), P())
    return jax.shard_map(
        body,
        mesh=mesh,
        in_specs=placed,
        out_specs=(P("ens", None, "lat", None), P("lat", "ens")),
        check_vma=False,
    )
```

```python
import math

import jax
import jax.numpy as jnp
import numpy as np
from jax import lax
from jax.experimental import pallas as pl
from jax.experimental.pallas import tpu as pltpu
from jax.sharding import PartitionSpec as P

SOFT2 = 0.1 * 0.1
CEILING = 2.0**60
SHRINK = 2.0 ** (-60)
LOG_SHIFT = 60.0 * math.log(2.0)
NLON, NLAT, DEG, MEM = 720, 384, 320, 16
GROUPS, VB = 5, 16
LANE = 128
MESH_AXES = ("ens", "lat")


def message_order(columns):
    row = lax.broadcasted_iota(jnp.int32, (LANE, LANE), 0)
    lane = lax.broadcasted_iota(jnp.int32, (LANE, LANE), 1)
    k, ahead = (row >> 4) & 3, (row & 15) - lane + 256 * (row >> 6)
    groups = []
    for g in range(GROUPS):
        extra = 80 if g < 3 else 160
        place = ahead + 16 * g + jnp.where(k < 2, k * LANE, jnp.where(k == 2, extra, -2048))
        tiles = [jnp.where(place == q * LANE, 1.0, 0.0) for q in range(columns)]
        groups.append(jnp.concatenate(tiles, axis=1).astype(jnp.bfloat16))
    return groups


def latitude_order():
    row = np.arange(256)
    jb, c = row // 8, row % 8
    return np.concatenate([12 * jb + c, 12 * jb + 8 + c // 2])


def dot(a, b, dims=((1,), (0,))):
    return lax.dot_general(a, b, (dims, ((), ())), preferred_element_type=jnp.float32)


STEP = math.pi / 360.0
SIN_TERMS = [(-1) ** n / math.factorial(2 * n + 1) * STEP ** (2 * n + 1) / math.sqrt(NLON) for n in range(6)]


def scaled_sine(steps):
    square = steps * steps
    total = SIN_TERMS[5]
    for term in SIN_TERMS[4::-1]:
        total = total * square + term
    return (total * steps).astype(jnp.bfloat16)


def fourier_blocks(wave):
    lon = lax.broadcasted_iota(jnp.int32, (32, NLON), 1).astype(jnp.float32)
    turn = wave * lon
    turn = turn - NLON * jnp.floor((turn + 0.5) * (1.0 / NLON)) - 360.0
    folded = jnp.maximum(jnp.minimum(turn, 360.0 - turn), -360.0 - turn)
    return scaled_sine(jnp.abs(turn) - 180.0), scaled_sine(folded)


def forward_kernel(wave_ref, members_hbm, analysis_hbm, sent_ref, table_ref, members, analysis, rows, sems):
    loads = [
        pltpu.make_async_copy(members_hbm, members, sems.at[0]),
        pltpu.make_async_copy(analysis_hbm, analysis, sems.at[1]),
    ]
    for load in loads:
        load.start()
    waves = jnp.broadcast_to(wave_ref[...].reshape(1, DEG).astype(jnp.float32), (32, DEG))
    ahead = lax.broadcasted_iota(jnp.int32, (32, DEG), 1) - 10 * lax.broadcasted_iota(jnp.int32, (32, DEG), 0)
    columns = [jnp.sum(jnp.where(ahead == k, waves, 0.0), axis=1, keepdims=True) for k in range(10)]
    for slot in range(10):
        for part, block in enumerate(fourier_blocks(columns[slot])):
            sb, g = divmod(2 * slot + part, GROUPS)
            at = g * LANE + sb * 32
            table_ref[at : at + 32, :] = block
    order = jnp.concatenate(message_order(4), axis=0)
    for load in loads:
        load.wait()

    deviation = (members[0].astype(jnp.float32) - analysis[...].astype(jnp.float32)).astype(jnp.bfloat16)
    blank = jnp.zeros((VB, NLON), jnp.bfloat16)
    for h in range(2):
        pieces = []
        for t in range(4):
            for vb in (2 * h, 2 * h + 1):
                pieces += [deviation[j, vb * VB : (vb + 1) * VB] for j in (2 * t, 2 * t + 1, 8 + t)] + [blank]
        fourier = dot(table_ref[...], jnp.concatenate(pieces, axis=0), ((1,), (1,))).astype(jnp.bfloat16)
        wide = jnp.concatenate(
            [
                jnp.concatenate(
                    [fourier[g * LANE : (g + 1) * LANE, t * LANE : (t + 1) * LANE] for g in range(GROUPS)],
                    axis=1,
                )
                for t in range(4)
            ],
            axis=0,
        )
        placed = dot(wide, order)
        for t in range(4):
            for q in range(4):
                at = (q // 2) * LANE * 8 + 2 * t + q % 2
                rows[pl.ds(at, LANE, stride=8), :] = placed[
                    t * LANE : (t + 1) * LANE, q * LANE : (q + 1) * LANE
                ]
        sent_ref[h * 256 : (h + 1) * 256] = rows[...].reshape(256, 8, LANE).astype(jnp.bfloat16)


def legendre_kernel(wave_ref, base_ref, cos_ref, logsin_ref, weight_ref, leg_ref, rows):
    wave = jnp.broadcast_to(wave_ref[...], (8, 512))
    wave2 = wave * wave
    cosine = jnp.broadcast_to(cos_ref[...], (8, 512))
    weight = jnp.broadcast_to(weight_ref[...], (8, 512))
    start_log = base_ref[...] + wave * logsin_ref[...]
    zero = jnp.zeros((8, 512), jnp.float32)

    def block(b, carry):
        for offset in range(8):
            previous, older, inverse, log_scale = carry
            index = b * 8 + offset
            degree = index.astype(jnp.float32)
            square = jnp.full((8, 512), degree * degree, jnp.float32)
            ratio = jnp.maximum(square - wave2, 1.0) / jnp.maximum(4.0 * square - 1.0, 1.0)
            factor = lax.rsqrt(ratio)
            current = factor * (cosine * previous - older * inverse)
            current = jnp.where(wave == degree, 1.0, current)
            too_large = jnp.abs(current) > CEILING
            shrink = jnp.where(too_large, SHRINK, 1.0)
            log_scale = jnp.where(too_large, log_scale + LOG_SHIFT, log_scale)
            current = current * shrink
            previous = previous * shrink
            value = weight * (current * jnp.exp(log_scale))
            for q in range(4):
                rows[q, pl.ds(pl.multiple_of(index * 8, 8), 8), :] = value[:, q * LANE : (q + 1) * LANE]
            carry = (current, previous, ratio * factor, log_scale)
        return carry

    lax.fori_loop(0, DEG // 8, block, (zero, zero, zero + 1.0, start_log))
    for s in range(3):
        for q in range(4):
            part = rows[q, pl.ds(s, DEG, stride=8), :]
            at = s * 512 + q * LANE
            leg_ref[:, at : at + LANE] = part.astype(jnp.bfloat16)


def pair_terms(z):
    pull = [None] * MEM
    inverse_sum = None
    for a in range(MEM):
        for b in range(a + 1, MEM):
            diff = z[a] - z[b]
            inverse = lax.rsqrt(diff * diff + SOFT2)
            term = diff * inverse
            inverse_sum = inverse if inverse_sum is None else inverse_sum + inverse
            pull[a] = term if pull[a] is None else pull[a] + term
            pull[b] = -term if pull[b] is None else pull[b] - term
    pair_abs = SOFT2 * inverse_sum
    single = None
    grads = []
    for e in range(MEM):
        square = z[e] * z[e] + SOFT2
        inverse = lax.rsqrt(square)
        soft = square * inverse
        single = soft if single is None else single + soft
        pair_abs = pair_abs + z[e] * pull[e]
        grads.append(z[e] * inverse - pull[e] * (1.0 / (MEM - 1)))
    pairs = MEM * (MEM - 1)
    return grads, (single - 0.1 * MEM) * (1.0 / MEM) - (pair_abs - 0.1 * (pairs // 2)) * (1.0 / pairs)


def score_kernel(got_ref, leg_ref, sent_ref, turned, coef, sums, scores):
    own_lat = lax.axis_index("lat")
    odd_block = lax.rem(lax.axis_index("ens"), 2)
    even = lax.broadcasted_iota(jnp.int32, (48, 256), 1) & 1 == 0
    unit = lax.broadcasted_iota(jnp.int32, (256, 256), 0) == lax.broadcasted_iota(jnp.int32, (256, 256), 1)
    unit = jnp.where(unit, 1.0, 0.0).astype(jnp.bfloat16)

    def slot_lanes(g):
        return pl.ds(pl.multiple_of((g + odd_block) // 2 * 512, 512), 512)

    def turn(member, _):
        message = got_ref[pl.ds(pl.multiple_of(member * 32, 32), 32)].astype(jnp.float32)
        message = message.reshape(256, LANE).astype(jnp.bfloat16)
        rows = dot(unit[:LANE, :LANE], message, ((1,), (1,)))
        at = pl.ds(pl.multiple_of(member * VB, VB), VB)
        low = jnp.where(even, rows[80:128], 0.0).astype(jnp.bfloat16)
        high = jnp.where(even, 0.0, rows[80:128]).astype(jnp.bfloat16)
        for g in range(GROUPS):
            turned[g, at, 0:256] = rows[g * VB : (g + 1) * VB].astype(jnp.bfloat16)
            extra = low[g * VB : (g + 1) * VB] if g < 3 else high[(g - 3) * VB : (g - 2) * VB]
            turned[g, at, 256:512] = extra
        return 0

    lax.fori_loop(0, MEM, turn, 0, unroll=4)

    first_half = lax.broadcasted_iota(jnp.int32, (8, LANE), 1) < 64

    def spectra(g):
        values = dot(turned[g], leg_ref[:, slot_lanes(g)], ((1,), (1,)))
        coef[g, :, 0:DEG] = values.astype(jnp.bfloat16).astype(jnp.float32)

    def score(g):
        for q in range(2):
            lanes = slice(q * LANE, (q + 1) * LANE)
            total = None
            for r in range(2):
                rows = [slice(e * VB + r * 8, e * VB + r * 8 + 8) for e in range(MEM)]
                grads, per = pair_terms([coef[g, row, lanes] for row in rows])
                for row, grad in zip(rows, grads):
                    coef[g, row, lanes] = grad
                total = per if total is None else total + per
            sums[g, :, lanes] = total
        lanes = slice(2 * LANE, 3 * LANE)
        packed = []
        for e in range(MEM):
            top, bottom = coef[g, e * VB : e * VB + 8, lanes], coef[g, e * VB + 8 : e * VB + VB, lanes]
            packed.append(jnp.where(first_half, top, pltpu.roll(bottom, 64, 1)))
        grads, per = pair_terms(packed)
        for e in range(MEM):
            coef[g, e * VB : e * VB + 8, lanes] = grads[e]
            coef[g, e * VB + 8 : e * VB + VB, lanes] = pltpu.roll(grads[e], 64, 1)
        sums[g, :, lanes] = per + pltpu.roll(per, 64, 1)

    def gradient(g):
        grad = coef[g, :, 0:DEG].astype(jnp.bfloat16)
        turned[g] = dot(grad, leg_ref[:, slot_lanes(g)]).astype(jnp.bfloat16)

    spectra(0)
    for g in range(GROUPS):
        if g + 1 < GROUPS:
            spectra(g + 1)
        score(g)
        gradient(g)

    place = lax.broadcasted_iota(jnp.int32, (16, DEG), 0)
    same = lax.rem(lax.broadcasted_iota(jnp.int32, (16, DEG), 1), 5) == lax.rem(place, 5)
    spread = jnp.zeros((16, DEG), jnp.float32)
    for g in range(GROUPS):
        mine = same & (place < 15) & (place // 5 == (g + odd_block) // 2)
        own = jnp.sum(sums[g], axis=0, keepdims=True)[:, 0:DEG]
        spread = spread + jnp.where(mine, jnp.broadcast_to(own, (16, DEG)), 0.0)
    spread = jnp.concatenate([jnp.zeros((112, DEG), jnp.float32), spread], axis=0).astype(jnp.bfloat16)
    out_row = lax.broadcasted_iota(jnp.int32, (LANE, DEG), 0)
    out_deg = lax.broadcasted_iota(jnp.int32, (LANE, DEG), 1)
    pick = (lax.rem(out_row, 2) == 1) & (out_deg // 5 == (out_row // 8) * 4 + lax.rem(out_row, 8) // 2)
    scores[...] = dot(jnp.where(pick, 1.0, 0.0).astype(jnp.bfloat16), spread, ((1,), (1,)))

    def send(pair, _):
        rows = []
        for k in range(2):
            at = pl.ds(pl.multiple_of((2 * pair + k) * VB, VB), VB)
            rows += [turned[g, at, 0:256] for g in range(GROUPS)]
            extra = [turned[g, at, 256:512].astype(jnp.float32) for g in range(GROUPS)]
            blank = jnp.zeros((VB, 256), jnp.float32)
            extra = jnp.where(even, jnp.concatenate(extra[:3]), jnp.concatenate(extra[3:] + [blank]))
            rows.append(extra.astype(jnp.bfloat16))
        back = dot(unit, jnp.concatenate(rows, axis=0), ((1,), (1,)))
        for k in range(2):
            member = 2 * pair + k
            message = back[:, k * LANE : (k + 1) * LANE].reshape(32, 8, LANE)
            sent_ref[pl.ds(pl.multiple_of(member * 32, 32), 32)] = message.astype(jnp.bfloat16)
            part = scores[pl.ds(pl.multiple_of(member * 8, 8), 8), :]
            own = member * 32 + own_lat
            sent_ref[own] = (sent_ref[own].astype(jnp.float32) + part).astype(jnp.bfloat16)
        return 0

    lax.fori_loop(0, MEM // 2, send, 0, unroll=2)


def inverse_kernel(got_ref, table_ref, grid_hbm, score_ref, rows, grid, sems):
    own_lat = lax.axis_index("lat")
    order = jnp.concatenate([group[0:48] for group in message_order(2)], axis=0)
    rows[...] = got_ref[...].astype(jnp.float32).reshape(512 * 8, LANE)
    turned = []
    for t in range(4):
        pair = [rows[pl.ds(2 * t + c, 512, stride=8), :].astype(jnp.bfloat16) for c in range(2)]
        turned.append(dot(order, jnp.concatenate(pair, axis=1), ((1,), (1,))).astype(jnp.bfloat16))
    stores = []
    for h in range(2):
        left = []
        for vb in (2 * h, 2 * h + 1):
            for t in range(4):
                left.append(
                    jnp.concatenate(
                        [turned[t][g * 48 : (g + 1) * 48, vb * LANE : (vb + 1) * LANE] for g in range(GROUPS)],
                        axis=1,
                    )
                )
        result = dot(jnp.concatenate(left, axis=0), table_ref[...]).astype(jnp.bfloat16)
        for vb in range(2):
            for t in range(4):
                for k, j in enumerate((2 * t, 2 * t + 1, 8 + t)):
                    at = (vb * 4 + t) * 48 + k * VB
                    grid[0, j, h * 32 + vb * VB : h * 32 + (vb + 1) * VB, :] = result[at : at + VB]
        half = (slice(None), slice(None), slice(h * 32, (h + 1) * 32), slice(None))
        stores.append(pltpu.make_async_copy(grid.at[half], grid_hbm.at[half], sems.at[h]))
        stores[-1].start()

    slot = lax.broadcasted_iota(jnp.int32, (16, LANE), 0)
    column = lax.broadcasted_iota(jnp.int32, (16, LANE), 1) - 112
    parts = [None] * 4
    for sb in range(4):
        tile = None
        for vb in range(4):
            piece = rows[pl.ds(pl.multiple_of((vb * LANE + sb * 32 + own_lat) * 8, 8), 8), :]
            tile = piece if tile is None else tile + piece
        here = (column >= 0) & (slot == (5 * sb) // 2 + (column + 5) // 5 - 1)
        for t in range(4):
            spread = jnp.where(here, jnp.broadcast_to(tile[2 * t + 1 : 2 * t + 2], (16, LANE)), 0.0)
            parts[t] = spread if parts[t] is None else parts[t] + spread
    source = lax.broadcasted_iota(jnp.int32, (512, LANE), 0)
    target = lax.broadcasted_iota(jnp.int32, (512, LANE), 1)
    inside = source % LANE - 110
    fits = (inside >= 2) & (inside < 17) & (target == 5 * (source // LANE) + (inside + 3) % 5)
    scores = lax.dot_general(
        jnp.concatenate(parts, axis=1),
        jnp.where(fits, 1.0, 0.0),
        (((1,), (0,)), ((), ())),
        precision=lax.Precision.HIGHEST,
        preferred_element_type=jnp.float32,
    )
    score_ref[...] = scores[:10, :20] * (1.0 / 128)
    for store in stores:
        store.wait()


def body(members, analysis, wave_order):
    mib = 1 << 20
    any_spec = pl.BlockSpec(memory_space=pltpu.HBM)
    vmem_spec = pl.BlockSpec(memory_space=pltpu.VMEM)
    waves = wave_order.astype(jnp.float32)
    sent, table = pl.pallas_call(
        forward_kernel,
        in_specs=[vmem_spec, any_spec, any_spec],
        out_shape=[
            jax.ShapeDtypeStruct((512, 8, LANE), jnp.bfloat16),
            jax.ShapeDtypeStruct((640, NLON), jnp.bfloat16),
        ],
        scratch_shapes=[
            pltpu.VMEM((1, 12, 64, NLON), jnp.bfloat16),
            pltpu.VMEM((12, 64, NLON), jnp.bfloat16),
            pltpu.VMEM((2048, LANE), jnp.float32),
            pltpu.SemaphoreType.DMA((2,)),
        ],
        compiler_params=pltpu.CompilerParams(vmem_limit_bytes=60 * mib),
        cost_estimate=pl.CostEstimate(flops=3 * 10**9, bytes_accessed=4 * 10**6, transcendentals=0),
        name="forward",
    )(wave_order, members.transpose(0, 2, 1, 3), analysis.transpose(1, 0, 2))
    got = lax.all_to_all(sent, MESH_AXES, 0, 0, tiled=True)

    own = lax.axis_index("lat") * 10 + (5 * lax.rem(lax.axis_index("ens"), 4)) // 2
    slots = lax.dynamic_slice_in_dim(waves, own, 3)
    slots = jnp.concatenate([slots, jnp.broadcast_to(slots[2:3], (5,))]).reshape(8, 1)
    base = 0.5 * (
        lax.lgamma(slots + 1.5) - lax.lgamma(slots + 1.0) - lax.lgamma(jnp.float32(1.5)) + math.log(0.5)
    )
    colatitude = (latitude_order() + 0.5) * (math.pi / NLAT)
    constants = [np.cos(colatitude), np.log(np.sin(colatitude)), math.sqrt(math.pi / NLAT) * np.sin(colatitude)]
    constants = [jnp.asarray(c[None].astype(np.float32)) for c in constants]
    legendre = pl.pallas_call(
        legendre_kernel,
        out_shape=jax.ShapeDtypeStruct((DEG, 1536), jnp.bfloat16),
        scratch_shapes=[pltpu.VMEM((4, DEG * 8, LANE), jnp.float32)],
        compiler_params=pltpu.CompilerParams(vmem_limit_bytes=16 * mib),
        cost_estimate=pl.CostEstimate(flops=10**8, bytes_accessed=2 * 10**6, transcendentals=3 * 10**6),
        name="legendre",
    )(slots, base, *constants)

    sent = pl.pallas_call(
        score_kernel,
        out_shape=jax.ShapeDtypeStruct((512, 8, LANE), jnp.bfloat16),
        scratch_shapes=[
            pltpu.VMEM((GROUPS, MEM * VB, 512), jnp.bfloat16),
            pltpu.VMEM((GROUPS, MEM * VB, 3 * LANE), jnp.float32),
            pltpu.VMEM((GROUPS, 8, 3 * LANE), jnp.float32),
            pltpu.VMEM((LANE, LANE), jnp.float32),
        ],
        compiler_params=pltpu.CompilerParams(vmem_limit_bytes=20 * mib),
        cost_estimate=pl.CostEstimate(flops=6 * 10**9, bytes_accessed=5 * 10**6, transcendentals=5 * 10**6),
        name="score",
    )(got, legendre)
    got = lax.all_to_all(sent, MESH_AXES, 0, 0, tiled=True)

    grid_grad, coef_score = pl.pallas_call(
        inverse_kernel,
        in_specs=[vmem_spec, vmem_spec],
        out_specs=[any_spec, vmem_spec],
        out_shape=[
            jax.ShapeDtypeStruct((1, 12, 64, NLON), jnp.bfloat16),
            jax.ShapeDtypeStruct((10, 20), jnp.float32),
        ],
        scratch_shapes=[
            pltpu.VMEM((4096, LANE), jnp.float32),
            pltpu.VMEM((1, 12, 64, NLON), jnp.bfloat16),
            pltpu.SemaphoreType.DMA((2,)),
        ],
        compiler_params=pltpu.CompilerParams(vmem_limit_bytes=24 * mib),
        cost_estimate=pl.CostEstimate(flops=2 * 10**9, bytes_accessed=4 * 10**6, transcendentals=0),
        name="inverse",
    )(got, table)
    return (grid_grad.transpose(0, 2, 1, 3), coef_score)


def solution(mesh):
    placed = (P("ens", None, "lat", None), P(None, "lat", None), P())
    return jax.shard_map(
        body,
        mesh=mesh,
        in_specs=placed,
        out_specs=(P("ens", None, "lat", None), P("lat", "ens")),
        check_vma=False,
    )
```

```python
import math

import jax
import jax.numpy as jnp
import numpy as np
from jax import lax
from jax.experimental import pallas as pl
from jax.experimental.pallas import tpu as pltpu
from jax.sharding import PartitionSpec as P

SOFT2 = 0.1 * 0.1
CEILING = 2.0**60
SHRINK = 2.0 ** (-60)
LOG_SHIFT = 60.0 * math.log(2.0)
NLON, NLAT, DEG, MEM = 720, 384, 320, 16
GROUPS, VB = 5, 16
LANE = 128
MESH_AXES = ("ens", "lat")


def message_order(columns):
    row = lax.broadcasted_iota(jnp.int32, (LANE, LANE), 0)
    lane = lax.broadcasted_iota(jnp.int32, (LANE, LANE), 1)
    k, ahead = (row >> 4) & 3, (row & 15) - lane + 256 * (row >> 6)
    groups = []
    for g in range(GROUPS):
        extra = 80 if g < 3 else 160
        place = ahead + 16 * g + jnp.where(k < 2, k * LANE, jnp.where(k == 2, extra, -2048))
        tiles = [jnp.where(place == q * LANE, 1.0, 0.0) for q in range(columns)]
        groups.append(jnp.concatenate(tiles, axis=1).astype(jnp.bfloat16))
    return groups


def latitude_order():
    row = np.arange(256)
    jb, c = row // 8, row % 8
    return np.concatenate([12 * jb + c, 12 * jb + 8 + c // 2])


def dot(a, b, dims=((1,), (0,))):
    return lax.dot_general(a, b, (dims, ((), ())), preferred_element_type=jnp.float32)


STEP = math.pi / 360.0
SIN_TERMS = [(-1) ** n / math.factorial(2 * n + 1) * STEP ** (2 * n + 1) / math.sqrt(NLON) for n in range(6)]


def scaled_sine(steps):
    square = steps * steps
    total = SIN_TERMS[5]
    for term in SIN_TERMS[4::-1]:
        total = total * square + term
    return (total * steps).astype(jnp.bfloat16)


def fourier_blocks(wave):
    lon = lax.broadcasted_iota(jnp.int32, (32, NLON), 1).astype(jnp.float32)
    turn = wave * lon
    turn = turn - NLON * jnp.floor((turn + 0.5) * (1.0 / NLON)) - 360.0
    folded = jnp.maximum(jnp.minimum(turn, 360.0 - turn), -360.0 - turn)
    return scaled_sine(jnp.abs(turn) - 180.0), scaled_sine(folded)


def forward_kernel(wave_ref, members_hbm, analysis_hbm, sent_ref, table_ref, members, analysis, rows, sems):
    loads = [
        pltpu.make_async_copy(members_hbm, members, sems.at[0]),
        pltpu.make_async_copy(analysis_hbm, analysis, sems.at[1]),
    ]
    for load in loads:
        load.start()
    waves = jnp.broadcast_to(wave_ref[...].reshape(1, DEG).astype(jnp.float32), (32, DEG))
    ahead = lax.broadcasted_iota(jnp.int32, (32, DEG), 1) - 10 * lax.broadcasted_iota(jnp.int32, (32, DEG), 0)
    columns = [jnp.sum(jnp.where(ahead == k, waves, 0.0), axis=1, keepdims=True) for k in range(10)]
    for slot in range(10):
        for part, block in enumerate(fourier_blocks(columns[slot])):
            sb, g = divmod(2 * slot + part, GROUPS)
            at = g * LANE + sb * 32
            table_ref[at : at + 32, :] = block
    order = jnp.concatenate(message_order(4), axis=0)
    for load in loads:
        load.wait()

    deviation = (members[0].astype(jnp.float32) - analysis[...].astype(jnp.float32)).astype(jnp.bfloat16)
    blank = jnp.zeros((VB, NLON), jnp.bfloat16)
    for h in range(2):
        pieces = []
        for t in range(4):
            for vb in (2 * h, 2 * h + 1):
                pieces += [deviation[j, vb * VB : (vb + 1) * VB] for j in (2 * t, 2 * t + 1, 8 + t)] + [blank]
        fourier = dot(table_ref[...], jnp.concatenate(pieces, axis=0), ((1,), (1,))).astype(jnp.bfloat16)
        wide = jnp.concatenate(
            [
                jnp.concatenate(
                    [fourier[g * LANE : (g + 1) * LANE, t * LANE : (t + 1) * LANE] for g in range(GROUPS)],
                    axis=1,
                )
                for t in range(4)
            ],
            axis=0,
        )
        placed = dot(wide, order)
        for t in range(4):
            for q in range(4):
                at = (q // 2) * LANE * 8 + 2 * t + q % 2
                rows[h, pl.ds(at, LANE, stride=8), :] = placed[
                    t * LANE : (t + 1) * LANE, q * LANE : (q + 1) * LANE
                ]
        sent_ref[h * 256 : (h + 1) * 256] = rows[h].reshape(256, 8, LANE).astype(jnp.bfloat16)


def legendre_kernel(wave_ref, base_ref, cos_ref, logsin_ref, weight_ref, leg_ref, rows):
    wave = jnp.broadcast_to(wave_ref[...], (8, 512))
    wave2 = wave * wave
    cosine = jnp.broadcast_to(cos_ref[...], (8, 512))
    weight = jnp.broadcast_to(weight_ref[...], (8, 512))
    start_log = base_ref[...] + wave * logsin_ref[...]
    zero = jnp.zeros((8, 512), jnp.float32)

    def block(b, carry):
        for offset in range(8):
            previous, older, inverse, log_scale = carry
            index = b * 8 + offset
            degree = index.astype(jnp.float32)
            square = jnp.full((8, 512), degree * degree, jnp.float32)
            ratio = jnp.maximum(square - wave2, 1.0) / jnp.maximum(4.0 * square - 1.0, 1.0)
            factor = lax.rsqrt(ratio)
            current = factor * (cosine * previous - older * inverse)
            current = jnp.where(wave == degree, 1.0, current)
            too_large = jnp.abs(current) > CEILING
            shrink = jnp.where(too_large, SHRINK, 1.0)
            log_scale = jnp.where(too_large, log_scale + LOG_SHIFT, log_scale)
            current = current * shrink
            previous = previous * shrink
            value = weight * (current * jnp.exp(log_scale))
            for q in range(4):
                rows[q, pl.ds(pl.multiple_of(index * 8, 8), 8), :] = value[:, q * LANE : (q + 1) * LANE]
            carry = (current, previous, ratio * factor, log_scale)
        return carry

    lax.fori_loop(0, DEG // 8, block, (zero, zero, zero + 1.0, start_log))
    for s in range(3):
        for q in range(4):
            part = rows[q, pl.ds(s, DEG, stride=8), :]
            at = s * 512 + q * LANE
            leg_ref[:, at : at + LANE] = part.astype(jnp.bfloat16)


def pair_terms(z):
    pull = [None] * MEM
    inverse_sum = None
    for a in range(MEM):
        for b in range(a + 1, MEM):
            diff = z[a] - z[b]
            inverse = lax.rsqrt(diff * diff + SOFT2)
            term = diff * inverse
            inverse_sum = inverse if inverse_sum is None else inverse_sum + inverse
            pull[a] = term if pull[a] is None else pull[a] + term
            pull[b] = -term if pull[b] is None else pull[b] - term
    pair_abs = SOFT2 * inverse_sum
    single = None
    grads = []
    for e in range(MEM):
        square = z[e] * z[e] + SOFT2
        inverse = lax.rsqrt(square)
        soft = square * inverse
        single = soft if single is None else single + soft
        pair_abs = pair_abs + z[e] * pull[e]
        grads.append(z[e] * inverse - pull[e] * (1.0 / (MEM - 1)))
    pairs = MEM * (MEM - 1)
    return grads, (single - 0.1 * MEM) * (1.0 / MEM) - (pair_abs - 0.1 * (pairs // 2)) * (1.0 / pairs)


def score_kernel(got_ref, leg_ref, sent_ref, turned, coef, sums, scores):
    own_lat = lax.axis_index("lat")
    odd_block = lax.rem(lax.axis_index("ens"), 2)
    even = lax.broadcasted_iota(jnp.int32, (48, 256), 1) & 1 == 0
    unit = lax.broadcasted_iota(jnp.int32, (256, 256), 0) == lax.broadcasted_iota(jnp.int32, (256, 256), 1)
    unit = jnp.where(unit, 1.0, 0.0).astype(jnp.bfloat16)

    def slot_lanes(g):
        return pl.ds(pl.multiple_of((g + odd_block) // 2 * 512, 512), 512)

    def turn(member, _):
        message = got_ref[pl.ds(pl.multiple_of(member * 32, 32), 32)].astype(jnp.float32)
        message = message.reshape(256, LANE).astype(jnp.bfloat16)
        rows = dot(unit[:LANE, :LANE], message, ((1,), (1,)))
        at = pl.ds(pl.multiple_of(member * VB, VB), VB)
        low = jnp.where(even, rows[80:128], 0.0).astype(jnp.bfloat16)
        high = jnp.where(even, 0.0, rows[80:128]).astype(jnp.bfloat16)
        for g in range(GROUPS):
            turned[g, at, 0:256] = rows[g * VB : (g + 1) * VB].astype(jnp.bfloat16)
            extra = low[g * VB : (g + 1) * VB] if g < 3 else high[(g - 3) * VB : (g - 2) * VB]
            turned[g, at, 256:512] = extra
        return 0

    lax.fori_loop(0, MEM, turn, 0, unroll=True)

    first_half = lax.broadcasted_iota(jnp.int32, (8, LANE), 1) < 64

    def spectra(g):
        values = dot(turned[g], leg_ref[:, slot_lanes(g)], ((1,), (1,)))
        coef[g, :, 0:DEG] = values.astype(jnp.bfloat16).astype(jnp.float32)

    def score(g):
        for q in range(2):
            lanes = slice(q * LANE, (q + 1) * LANE)
            total = None
            for r in range(2):
                rows = [slice(e * VB + r * 8, e * VB + r * 8 + 8) for e in range(MEM)]
                grads, per = pair_terms([coef[g, row, lanes] for row in rows])
                for row, grad in zip(rows, grads):
                    coef[g, row, lanes] = grad
                total = per if total is None else total + per
            sums[g, :, lanes] = total
        lanes = slice(2 * LANE, 3 * LANE)
        packed = []
        for e in range(MEM):
            top, bottom = coef[g, e * VB : e * VB + 8, lanes], coef[g, e * VB + 8 : e * VB + VB, lanes]
            packed.append(jnp.where(first_half, top, pltpu.roll(bottom, 64, 1)))
        grads, per = pair_terms(packed)
        for e in range(MEM):
            coef[g, e * VB : e * VB + 8, lanes] = grads[e]
            coef[g, e * VB + 8 : e * VB + VB, lanes] = pltpu.roll(grads[e], 64, 1)
        sums[g, :, lanes] = per + pltpu.roll(per, 64, 1)

    def gradient(g):
        grad = coef[g, :, 0:DEG].astype(jnp.bfloat16)
        turned[g] = dot(grad, leg_ref[:, slot_lanes(g)]).astype(jnp.bfloat16)

    spectra(0)
    for g in range(GROUPS):
        if g + 1 < GROUPS:
            spectra(g + 1)
        score(g)
        gradient(g)

    place = lax.broadcasted_iota(jnp.int32, (16, DEG), 0)
    same = lax.rem(lax.broadcasted_iota(jnp.int32, (16, DEG), 1), 5) == lax.rem(place, 5)
    spread = jnp.zeros((16, DEG), jnp.float32)
    for g in range(GROUPS):
        mine = same & (place < 15) & (place // 5 == (g + odd_block) // 2)
        own = jnp.sum(sums[g], axis=0, keepdims=True)[:, 0:DEG]
        spread = spread + jnp.where(mine, jnp.broadcast_to(own, (16, DEG)), 0.0)
    spread = jnp.concatenate([jnp.zeros((112, DEG), jnp.float32), spread], axis=0).astype(jnp.bfloat16)
    out_row = lax.broadcasted_iota(jnp.int32, (LANE, DEG), 0)
    out_deg = lax.broadcasted_iota(jnp.int32, (LANE, DEG), 1)
    pick = (lax.rem(out_row, 2) == 1) & (out_deg // 5 == (out_row // 8) * 4 + lax.rem(out_row, 8) // 2)
    scores[...] = dot(jnp.where(pick, 1.0, 0.0).astype(jnp.bfloat16), spread, ((1,), (1,)))

    def send(pair, _):
        rows = []
        for k in range(2):
            at = pl.ds(pl.multiple_of((2 * pair + k) * VB, VB), VB)
            rows += [turned[g, at, 0:256] for g in range(GROUPS)]
            extra = [turned[g, at, 256:512].astype(jnp.float32) for g in range(GROUPS)]
            blank = jnp.zeros((VB, 256), jnp.float32)
            extra = jnp.where(even, jnp.concatenate(extra[:3]), jnp.concatenate(extra[3:] + [blank]))
            rows.append(extra.astype(jnp.bfloat16))
        back = dot(unit, jnp.concatenate(rows, axis=0), ((1,), (1,)))
        for k in range(2):
            member = 2 * pair + k
            message = back[:, k * LANE : (k + 1) * LANE].reshape(32, 8, LANE)
            sent_ref[pl.ds(pl.multiple_of(member * 32, 32), 32)] = message.astype(jnp.bfloat16)
            part = scores[pl.ds(pl.multiple_of(member * 8, 8), 8), :]
            own = member * 32 + own_lat
            sent_ref[own] = (sent_ref[own].astype(jnp.float32) + part).astype(jnp.bfloat16)
        return 0

    lax.fori_loop(0, MEM // 2, send, 0, unroll=True)


def inverse_kernel(got_ref, table_ref, grid_hbm, score_ref, rows, grid, sems):
    own_lat = lax.axis_index("lat")
    order = jnp.concatenate([group[0:48] for group in message_order(2)], axis=0)
    rows[...] = got_ref[...].astype(jnp.float32).reshape(512 * 8, LANE)
    turned = []
    for t in range(4):
        pair = [rows[pl.ds(2 * t + c, 512, stride=8), :].astype(jnp.bfloat16) for c in range(2)]
        turned.append(dot(order, jnp.concatenate(pair, axis=1), ((1,), (1,))).astype(jnp.bfloat16))
    stores = []
    for h in range(2):
        left = []
        for vb in (2 * h, 2 * h + 1):
            for t in range(4):
                left.append(
                    jnp.concatenate(
                        [turned[t][g * 48 : (g + 1) * 48, vb * LANE : (vb + 1) * LANE] for g in range(GROUPS)],
                        axis=1,
                    )
                )
        result = dot(jnp.concatenate(left, axis=0), table_ref[...]).astype(jnp.bfloat16)
        for vb in range(2):
            for t in range(4):
                for k, j in enumerate((2 * t, 2 * t + 1, 8 + t)):
                    at = (vb * 4 + t) * 48 + k * VB
                    grid[0, j, h * 32 + vb * VB : h * 32 + (vb + 1) * VB, :] = result[at : at + VB]
        half = (slice(None), slice(None), slice(h * 32, (h + 1) * 32), slice(None))
        stores.append(pltpu.make_async_copy(grid.at[half], grid_hbm.at[half], sems.at[h]))
        stores[-1].start()

    slot = lax.broadcasted_iota(jnp.int32, (16, LANE), 0)
    column = lax.broadcasted_iota(jnp.int32, (16, LANE), 1) - 112
    parts = [None] * 4
    for sb in range(4):
        tile = None
        for vb in range(4):
            piece = rows[pl.ds(pl.multiple_of((vb * LANE + sb * 32 + own_lat) * 8, 8), 8), :]
            tile = piece if tile is None else tile + piece
        here = (column >= 0) & (slot == (5 * sb) // 2 + (column + 5) // 5 - 1)
        for t in range(4):
            spread = jnp.where(here, jnp.broadcast_to(tile[2 * t + 1 : 2 * t + 2], (16, LANE)), 0.0)
            parts[t] = spread if parts[t] is None else parts[t] + spread
    source = lax.broadcasted_iota(jnp.int32, (512, LANE), 0)
    target = lax.broadcasted_iota(jnp.int32, (512, LANE), 1)
    inside = source % LANE - 110
    fits = (inside >= 2) & (inside < 17) & (target == 5 * (source // LANE) + (inside + 3) % 5)
    scores = lax.dot_general(
        jnp.concatenate(parts, axis=1),
        jnp.where(fits, 1.0, 0.0),
        (((1,), (0,)), ((), ())),
        precision=lax.Precision.HIGHEST,
        preferred_element_type=jnp.float32,
    )
    score_ref[...] = scores[:10, :20] * (1.0 / 128)
    for store in stores:
        store.wait()


def body(members, analysis, wave_order):
    mib = 1 << 20
    any_spec = pl.BlockSpec(memory_space=pltpu.HBM)
    vmem_spec = pl.BlockSpec(memory_space=pltpu.VMEM)
    waves = wave_order.astype(jnp.float32)
    sent, table = pl.pallas_call(
        forward_kernel,
        in_specs=[vmem_spec, any_spec, any_spec],
        out_shape=[
            jax.ShapeDtypeStruct((512, 8, LANE), jnp.bfloat16),
            jax.ShapeDtypeStruct((640, NLON), jnp.bfloat16),
        ],
        scratch_shapes=[
            pltpu.VMEM((1, 12, 64, NLON), jnp.bfloat16),
            pltpu.VMEM((12, 64, NLON), jnp.bfloat16),
            pltpu.VMEM((2, 2048, LANE), jnp.float32),
            pltpu.SemaphoreType.DMA((2,)),
        ],
        compiler_params=pltpu.CompilerParams(vmem_limit_bytes=60 * mib),
        cost_estimate=pl.CostEstimate(flops=3 * 10**9, bytes_accessed=4 * 10**6, transcendentals=0),
        name="forward",
    )(wave_order, members.transpose(0, 2, 1, 3), analysis.transpose(1, 0, 2))
    got = lax.all_to_all(sent, MESH_AXES, 0, 0, tiled=True)

    own = lax.axis_index("lat") * 10 + (5 * lax.rem(lax.axis_index("ens"), 4)) // 2
    slots = lax.dynamic_slice_in_dim(waves, own, 3)
    slots = jnp.concatenate([slots, jnp.broadcast_to(slots[2:3], (5,))]).reshape(8, 1)
    base = 0.5 * (
        lax.lgamma(slots + 1.5) - lax.lgamma(slots + 1.0) - lax.lgamma(jnp.float32(1.5)) + math.log(0.5)
    )
    colatitude = (latitude_order() + 0.5) * (math.pi / NLAT)
    constants = [np.cos(colatitude), np.log(np.sin(colatitude)), math.sqrt(math.pi / NLAT) * np.sin(colatitude)]
    constants = [jnp.asarray(c[None].astype(np.float32)) for c in constants]
    legendre = pl.pallas_call(
        legendre_kernel,
        out_shape=jax.ShapeDtypeStruct((DEG, 1536), jnp.bfloat16),
        scratch_shapes=[pltpu.VMEM((4, DEG * 8, LANE), jnp.float32)],
        compiler_params=pltpu.CompilerParams(vmem_limit_bytes=16 * mib),
        cost_estimate=pl.CostEstimate(flops=10**8, bytes_accessed=2 * 10**6, transcendentals=3 * 10**6),
        name="legendre",
    )(slots, base, *constants)

    sent = pl.pallas_call(
        score_kernel,
        out_shape=jax.ShapeDtypeStruct((512, 8, LANE), jnp.bfloat16),
        scratch_shapes=[
            pltpu.VMEM((GROUPS, MEM * VB, 512), jnp.bfloat16),
            pltpu.VMEM((GROUPS, MEM * VB, 3 * LANE), jnp.float32),
            pltpu.VMEM((GROUPS, 8, 3 * LANE), jnp.float32),
            pltpu.VMEM((LANE, LANE), jnp.float32),
        ],
        compiler_params=pltpu.CompilerParams(vmem_limit_bytes=20 * mib),
        cost_estimate=pl.CostEstimate(flops=6 * 10**9, bytes_accessed=5 * 10**6, transcendentals=5 * 10**6),
        name="score",
    )(got, legendre)
    got = lax.all_to_all(sent, MESH_AXES, 0, 0, tiled=True)

    grid_grad, coef_score = pl.pallas_call(
        inverse_kernel,
        in_specs=[vmem_spec, vmem_spec],
        out_specs=[any_spec, vmem_spec],
        out_shape=[
            jax.ShapeDtypeStruct((1, 12, 64, NLON), jnp.bfloat16),
            jax.ShapeDtypeStruct((10, 20), jnp.float32),
        ],
        scratch_shapes=[
            pltpu.VMEM((4096, LANE), jnp.float32),
            pltpu.VMEM((1, 12, 64, NLON), jnp.bfloat16),
            pltpu.SemaphoreType.DMA((2,)),
        ],
        compiler_params=pltpu.CompilerParams(vmem_limit_bytes=24 * mib),
        cost_estimate=pl.CostEstimate(flops=2 * 10**9, bytes_accessed=4 * 10**6, transcendentals=0),
        name="inverse",
    )(got, table)
    return (grid_grad.transpose(0, 2, 1, 3), coef_score)


def solution(mesh):
    placed = (P("ens", None, "lat", None), P(None, "lat", None), P())
    return jax.shard_map(
        body,
        mesh=mesh,
        in_specs=placed,
        out_specs=(P("ens", None, "lat", None), P("lat", "ens")),
        check_vma=False,
    )
```

```python
import math

import jax
import jax.numpy as jnp
import numpy as np
from jax import lax
from jax.experimental import pallas as pl
from jax.experimental.pallas import tpu as pltpu
from jax.sharding import PartitionSpec as P

SOFT2 = 0.1 * 0.1
CEILING = 2.0**60
SHRINK = 2.0 ** (-60)
LOG_SHIFT = 60.0 * math.log(2.0)
NLON, NLAT, DEG, MEM = 720, 384, 320, 16
GROUPS, VB = 5, 16
LANE = 128
MESH_AXES = ("ens", "lat")


def message_order(columns):
    row = lax.broadcasted_iota(jnp.int32, (LANE, LANE), 0)
    lane = lax.broadcasted_iota(jnp.int32, (LANE, LANE), 1)
    k, ahead = (row >> 4) & 3, (row & 15) - lane + 256 * (row >> 6)
    groups = []
    for g in range(GROUPS):
        extra = 80 if g < 3 else 160
        place = ahead + 16 * g + jnp.where(k < 2, k * LANE, jnp.where(k == 2, extra, -2048))
        tiles = [jnp.where(place == q * LANE, 1.0, 0.0) for q in range(columns)]
        groups.append(jnp.concatenate(tiles, axis=1).astype(jnp.bfloat16))
    return groups


def latitude_order():
    row = np.arange(256)
    jb, c = row // 8, row % 8
    return np.concatenate([12 * jb + c, 12 * jb + 8 + c // 2])


def dot(a, b, dims=((1,), (0,))):
    return lax.dot_general(a, b, (dims, ((), ())), preferred_element_type=jnp.float32)


STEP = math.pi / 360.0
SIN_TERMS = [(-1) ** n / math.factorial(2 * n + 1) * STEP ** (2 * n + 1) / math.sqrt(NLON) for n in range(6)]


def scaled_sine(steps):
    square = steps * steps
    total = SIN_TERMS[5]
    for term in SIN_TERMS[4::-1]:
        total = total * square + term
    return (total * steps).astype(jnp.bfloat16)


def fourier_blocks(wave):
    lon = lax.broadcasted_iota(jnp.int32, (32, NLON), 1).astype(jnp.float32)
    turn = wave * lon
    turn = turn - NLON * jnp.floor((turn + 0.5) * (1.0 / NLON)) - 360.0
    folded = jnp.maximum(jnp.minimum(turn, 360.0 - turn), -360.0 - turn)
    return scaled_sine(jnp.abs(turn) - 180.0), scaled_sine(folded)


def forward_kernel(
    wave_ref, members_hbm, analysis_hbm, sent_hbm, table_hbm, members, analysis, rows, sent_ref, table_ref, sems
):
    loads = [
        pltpu.make_async_copy(members_hbm, members, sems.at[0]),
        pltpu.make_async_copy(analysis_hbm, analysis, sems.at[1]),
    ]
    for load in loads:
        load.start()
    waves = jnp.broadcast_to(wave_ref[...].reshape(1, DEG).astype(jnp.float32), (32, DEG))
    ahead = lax.broadcasted_iota(jnp.int32, (32, DEG), 1) - 10 * lax.broadcasted_iota(jnp.int32, (32, DEG), 0)
    columns = [jnp.sum(jnp.where(ahead == k, waves, 0.0), axis=1, keepdims=True) for k in range(10)]
    for slot in range(10):
        for part, block in enumerate(fourier_blocks(columns[slot])):
            sb, g = divmod(2 * slot + part, GROUPS)
            at = g * LANE + sb * 32
            table_ref[at : at + 32, :] = block
    stores = [pltpu.make_async_copy(table_ref, table_hbm, sems.at[2])]
    stores[0].start()
    order = jnp.concatenate(message_order(4), axis=0)
    for load in loads:
        load.wait()

    deviation = (members[0].astype(jnp.float32) - analysis[...].astype(jnp.float32)).astype(
        jnp.bfloat16
    )
    blank = jnp.zeros((VB, NLON), jnp.bfloat16)
    for h in range(2):
        pieces = []
        for t in range(4):
            for vb in (2 * h, 2 * h + 1):
                pieces += [deviation[j, vb * VB : (vb + 1) * VB] for j in (2 * t, 2 * t + 1, 8 + t)] + [blank]
        fourier = dot(table_ref[...], jnp.concatenate(pieces, axis=0), ((1,), (1,))).astype(jnp.bfloat16)
        wide = jnp.concatenate(
            [
                jnp.concatenate(
                    [fourier[g * LANE : (g + 1) * LANE, t * LANE : (t + 1) * LANE] for g in range(GROUPS)],
                    axis=1,
                )
                for t in range(4)
            ],
            axis=0,
        )
        placed = dot(wide, order)
        for t in range(4):
            for q in range(4):
                at = (q // 2) * LANE * 8 + 2 * t + q % 2
                rows[h, pl.ds(at, LANE, stride=8), :] = placed[
                    t * LANE : (t + 1) * LANE, q * LANE : (q + 1) * LANE
                ]
        sent_ref[h * 256 : (h + 1) * 256] = rows[h].reshape(256, 8, LANE).astype(jnp.bfloat16)
        half = pl.ds(h * 256, 256)
        stores.append(pltpu.make_async_copy(sent_ref.at[half], sent_hbm.at[half], sems.at[3 + h]))
        stores[-1].start()
    for store in stores:
        store.wait()


def legendre_kernel(wave_ref, base_ref, cos_ref, logsin_ref, weight_ref, leg_ref, rows):
    wave = jnp.broadcast_to(wave_ref[...], (8, 512))
    wave2 = wave * wave
    cosine = jnp.broadcast_to(cos_ref[...], (8, 512))
    weight = jnp.broadcast_to(weight_ref[...], (8, 512))
    start_log = base_ref[...] + wave * logsin_ref[...]
    zero = jnp.zeros((8, 512), jnp.float32)

    def block(b, carry):
        for offset in range(8):
            previous, older, inverse, log_scale = carry
            index = b * 8 + offset
            degree = index.astype(jnp.float32)
            square = jnp.full((8, 512), degree * degree, jnp.float32)
            ratio = jnp.maximum(square - wave2, 1.0) / jnp.maximum(4.0 * square - 1.0, 1.0)
            factor = lax.rsqrt(ratio)
            current = factor * (cosine * previous - older * inverse)
            current = jnp.where(wave == degree, 1.0, current)
            too_large = jnp.abs(current) > CEILING
            shrink = jnp.where(too_large, SHRINK, 1.0)
            log_scale = jnp.where(too_large, log_scale + LOG_SHIFT, log_scale)
            current = current * shrink
            previous = previous * shrink
            value = weight * (current * jnp.exp(log_scale))
            for q in range(4):
                rows[q, pl.ds(pl.multiple_of(index * 8, 8), 8), :] = value[:, q * LANE : (q + 1) * LANE]
            carry = (current, previous, ratio * factor, log_scale)
        return carry

    lax.fori_loop(0, DEG // 8, block, (zero, zero, zero + 1.0, start_log))
    for s in range(3):
        for q in range(4):
            part = rows[q, pl.ds(s, DEG, stride=8), :]
            at = s * 512 + q * LANE
            leg_ref[:, at : at + LANE] = part.astype(jnp.bfloat16)


def pair_terms(z):
    pull = [None] * MEM
    inverse_sum = None
    for a in range(MEM):
        for b in range(a + 1, MEM):
            diff = z[a] - z[b]
            inverse = lax.rsqrt(diff * diff + SOFT2)
            term = diff * inverse
            inverse_sum = inverse if inverse_sum is None else inverse_sum + inverse
            pull[a] = term if pull[a] is None else pull[a] + term
            pull[b] = -term if pull[b] is None else pull[b] - term
    pair_abs = SOFT2 * inverse_sum
    single = None
    grads = []
    for e in range(MEM):
        square = z[e] * z[e] + SOFT2
        inverse = lax.rsqrt(square)
        soft = square * inverse
        single = soft if single is None else single + soft
        pair_abs = pair_abs + z[e] * pull[e]
        grads.append(z[e] * inverse - pull[e] * (1.0 / (MEM - 1)))
    pairs = MEM * (MEM - 1)
    return grads, (single - 0.1 * MEM) * (1.0 / MEM) - (pair_abs - 0.1 * (pairs // 2)) * (1.0 / pairs)


def score_kernel(got_ref, leg_ref, sent_ref, turned, coef, sums, scores):
    own_lat = lax.axis_index("lat")
    odd_block = lax.rem(lax.axis_index("ens"), 2)
    even = lax.broadcasted_iota(jnp.int32, (48, 256), 1) & 1 == 0
    unit = lax.broadcasted_iota(jnp.int32, (256, 256), 0) == lax.broadcasted_iota(jnp.int32, (256, 256), 1)
    unit = jnp.where(unit, 1.0, 0.0).astype(jnp.bfloat16)

    def slot_lanes(g):
        return pl.ds(pl.multiple_of((g + odd_block) // 2 * 512, 512), 512)

    def turn(pair, _):
        messages = []
        for k in range(2):
            message = got_ref[pl.ds(pl.multiple_of((2 * pair + k) * 32, 32), 32)].astype(jnp.float32)
            messages.append(message.reshape(256, LANE).astype(jnp.bfloat16))
        both = dot(unit, jnp.concatenate(messages, axis=1), ((1,), (1,)))
        for k in range(2):
            rows = both[k * LANE : (k + 1) * LANE]
            at = pl.ds(pl.multiple_of((2 * pair + k) * VB, VB), VB)
            low = jnp.where(even, rows[80:128], 0.0).astype(jnp.bfloat16)
            high = jnp.where(even, 0.0, rows[80:128]).astype(jnp.bfloat16)
            for g in range(GROUPS):
                turned[g, at, 0:256] = rows[g * VB : (g + 1) * VB].astype(jnp.bfloat16)
                extra = low[g * VB : (g + 1) * VB] if g < 3 else high[(g - 3) * VB : (g - 2) * VB]
                turned[g, at, 256:512] = extra
        return 0

    lax.fori_loop(0, MEM // 2, turn, 0, unroll=True)

    first_half = lax.broadcasted_iota(jnp.int32, (8, LANE), 1) < 64

    def spectra(g):
        values = dot(turned[g], leg_ref[:, slot_lanes(g)], ((1,), (1,)))
        coef[g, :, 0:DEG] = values.astype(jnp.bfloat16).astype(jnp.float32)

    def score(g):
        for q in range(2):
            lanes = slice(q * LANE, (q + 1) * LANE)
            total = None
            for r in range(2):
                rows = [slice(e * VB + r * 8, e * VB + r * 8 + 8) for e in range(MEM)]
                grads, per = pair_terms([coef[g, row, lanes] for row in rows])
                for row, grad in zip(rows, grads):
                    coef[g, row, lanes] = grad
                total = per if total is None else total + per
            sums[g, :, lanes] = total
        lanes = slice(2 * LANE, 3 * LANE)
        packed = []
        for e in range(MEM):
            top, bottom = coef[g, e * VB : e * VB + 8, lanes], coef[g, e * VB + 8 : e * VB + VB, lanes]
            packed.append(jnp.where(first_half, top, pltpu.roll(bottom, 64, 1)))
        grads, per = pair_terms(packed)
        for e in range(MEM):
            coef[g, e * VB : e * VB + 8, lanes] = grads[e]
            coef[g, e * VB + 8 : e * VB + VB, lanes] = pltpu.roll(grads[e], 64, 1)
        sums[g, :, lanes] = per + pltpu.roll(per, 64, 1)

    def gradient(g):
        grad = coef[g, :, 0:DEG].astype(jnp.bfloat16)
        turned[g] = dot(grad, leg_ref[:, slot_lanes(g)]).astype(jnp.bfloat16)

    spectra(0)
    for g in range(GROUPS):
        if g + 1 < GROUPS:
            spectra(g + 1)
        score(g)
        gradient(g)

    place = lax.broadcasted_iota(jnp.int32, (16, DEG), 0)
    same = lax.rem(lax.broadcasted_iota(jnp.int32, (16, DEG), 1), 5) == lax.rem(place, 5)
    spread = jnp.zeros((16, DEG), jnp.float32)
    for g in range(GROUPS):
        mine = same & (place < 15) & (place // 5 == (g + odd_block) // 2)
        own = jnp.sum(sums[g], axis=0, keepdims=True)[:, 0:DEG]
        spread = spread + jnp.where(mine, jnp.broadcast_to(own, (16, DEG)), 0.0)
    spread = jnp.concatenate([jnp.zeros((112, DEG), jnp.float32), spread], axis=0).astype(jnp.bfloat16)
    out_row = lax.broadcasted_iota(jnp.int32, (LANE, DEG), 0)
    out_deg = lax.broadcasted_iota(jnp.int32, (LANE, DEG), 1)
    pick = (lax.rem(out_row, 2) == 1) & (out_deg // 5 == (out_row // 8) * 4 + lax.rem(out_row, 8) // 2)
    scores[...] = dot(jnp.where(pick, 1.0, 0.0).astype(jnp.bfloat16), spread, ((1,), (1,)))

    def send(pair, _):
        rows = []
        for k in range(2):
            at = pl.ds(pl.multiple_of((2 * pair + k) * VB, VB), VB)
            rows += [turned[g, at, 0:256] for g in range(GROUPS)]
            extra = [turned[g, at, 256:512].astype(jnp.float32) for g in range(GROUPS)]
            blank = jnp.zeros((VB, 256), jnp.float32)
            extra = jnp.where(even, jnp.concatenate(extra[:3]), jnp.concatenate(extra[3:] + [blank]))
            rows.append(extra.astype(jnp.bfloat16))
        back = dot(unit, jnp.concatenate(rows, axis=0), ((1,), (1,)))
        for k in range(2):
            member = 2 * pair + k
            message = back[:, k * LANE : (k + 1) * LANE].reshape(32, 8, LANE)
            sent_ref[pl.ds(pl.multiple_of(member * 32, 32), 32)] = message.astype(jnp.bfloat16)
            part = scores[pl.ds(pl.multiple_of(member * 8, 8), 8), :]
            own = member * 32 + own_lat
            sent_ref[own] = (sent_ref[own].astype(jnp.float32) + part).astype(jnp.bfloat16)
        return 0

    lax.fori_loop(0, MEM // 2, send, 0, unroll=True)


def inverse_kernel(got_ref, table_ref, grid_hbm, score_ref, rows, grid, sems):
    own_lat = lax.axis_index("lat")
    order = jnp.concatenate([group[0:48] for group in message_order(2)], axis=0)
    rows[...] = got_ref[...].astype(jnp.float32).reshape(512 * 8, LANE)
    turned = []
    for t in range(4):
        pair = [rows[pl.ds(2 * t + c, 512, stride=8), :].astype(jnp.bfloat16) for c in range(2)]
        turned.append(dot(order, jnp.concatenate(pair, axis=1), ((1,), (1,))).astype(jnp.bfloat16))
    stores = []
    for h in range(2):
        left = []
        for vb in (2 * h, 2 * h + 1):
            for t in range(4):
                left.append(
                    jnp.concatenate(
                        [turned[t][g * 48 : (g + 1) * 48, vb * LANE : (vb + 1) * LANE] for g in range(GROUPS)],
                        axis=1,
                    )
                )
        result = dot(jnp.concatenate(left, axis=0), table_ref[...]).astype(jnp.bfloat16)
        for vb in range(2):
            for t in range(4):
                for k, j in enumerate((2 * t, 2 * t + 1, 8 + t)):
                    at = (vb * 4 + t) * 48 + k * VB
                    grid[0, j, h * 32 + vb * VB : h * 32 + (vb + 1) * VB, :] = result[at : at + VB]
        half = (slice(None), slice(None), slice(h * 32, (h + 1) * 32), slice(None))
        stores.append(pltpu.make_async_copy(grid.at[half], grid_hbm.at[half], sems.at[h]))
        stores[-1].start()

    slot = lax.broadcasted_iota(jnp.int32, (16, LANE), 0)
    column = lax.broadcasted_iota(jnp.int32, (16, LANE), 1) - 112
    parts = [None] * 4
    for sb in range(4):
        tile = None
        for vb in range(4):
            piece = rows[pl.ds(pl.multiple_of((vb * LANE + sb * 32 + own_lat) * 8, 8), 8), :]
            tile = piece if tile is None else tile + piece
        here = (column >= 0) & (slot == (5 * sb) // 2 + (column + 5) // 5 - 1)
        for t in range(4):
            spread = jnp.where(here, jnp.broadcast_to(tile[2 * t + 1 : 2 * t + 2], (16, LANE)), 0.0)
            parts[t] = spread if parts[t] is None else parts[t] + spread
    source = lax.broadcasted_iota(jnp.int32, (512, LANE), 0)
    target = lax.broadcasted_iota(jnp.int32, (512, LANE), 1)
    inside = source % LANE - 110
    fits = (inside >= 2) & (inside < 17) & (target == 5 * (source // LANE) + (inside + 3) % 5)
    scores = lax.dot_general(
        jnp.concatenate(parts, axis=1),
        jnp.where(fits, 1.0, 0.0),
        (((1,), (0,)), ((), ())),
        precision=lax.Precision.HIGHEST,
        preferred_element_type=jnp.float32,
    )
    score_ref[...] = scores[:10, :20] * (1.0 / 128)
    for store in stores:
        store.wait()


def body(members, analysis, wave_order):
    mib = 1 << 20
    any_spec = pl.BlockSpec(memory_space=pltpu.HBM)
    vmem_spec = pl.BlockSpec(memory_space=pltpu.VMEM)
    waves = wave_order.astype(jnp.float32)
    sent, table = pl.pallas_call(
        forward_kernel,
        in_specs=[vmem_spec, any_spec, any_spec],
        out_specs=[any_spec, any_spec],
        out_shape=[
            jax.ShapeDtypeStruct((512, 8, LANE), jnp.bfloat16),
            jax.ShapeDtypeStruct((640, NLON), jnp.bfloat16),
        ],
        scratch_shapes=[
            pltpu.VMEM((1, 12, 64, NLON), jnp.bfloat16),
            pltpu.VMEM((12, 64, NLON), jnp.bfloat16),
            pltpu.VMEM((2, 2048, LANE), jnp.float32),
            pltpu.VMEM((512, 8, LANE), jnp.bfloat16),
            pltpu.VMEM((640, NLON), jnp.bfloat16),
            pltpu.SemaphoreType.DMA((5,)),
        ],
        compiler_params=pltpu.CompilerParams(vmem_limit_bytes=60 * mib),
        cost_estimate=pl.CostEstimate(flops=3 * 10**9, bytes_accessed=4 * 10**6, transcendentals=0),
        name="forward",
    )(wave_order, members.transpose(0, 2, 1, 3), analysis.transpose(1, 0, 2))
    got = lax.all_to_all(sent, MESH_AXES, 0, 0, tiled=True)

    own = lax.axis_index("lat") * 10 + (5 * lax.rem(lax.axis_index("ens"), 4)) // 2
    slots = lax.dynamic_slice_in_dim(waves, own, 3)
    slots = jnp.concatenate([slots, jnp.broadcast_to(slots[2:3], (5,))]).reshape(8, 1)
    base = 0.5 * (
        lax.lgamma(slots + 1.5) - lax.lgamma(slots + 1.0) - lax.lgamma(jnp.float32(1.5)) + math.log(0.5)
    )
    colatitude = (latitude_order() + 0.5) * (math.pi / NLAT)
    constants = [np.cos(colatitude), np.log(np.sin(colatitude)), math.sqrt(math.pi / NLAT) * np.sin(colatitude)]
    constants = [jnp.asarray(c[None].astype(np.float32)) for c in constants]
    legendre = pl.pallas_call(
        legendre_kernel,
        out_shape=jax.ShapeDtypeStruct((DEG, 1536), jnp.bfloat16),
        scratch_shapes=[pltpu.VMEM((4, DEG * 8, LANE), jnp.float32)],
        compiler_params=pltpu.CompilerParams(vmem_limit_bytes=16 * mib),
        cost_estimate=pl.CostEstimate(flops=10**8, bytes_accessed=2 * 10**6, transcendentals=3 * 10**6),
        name="legendre",
    )(slots, base, *constants)

    sent = pl.pallas_call(
        score_kernel,
        out_shape=jax.ShapeDtypeStruct((512, 8, LANE), jnp.bfloat16),
        scratch_shapes=[
            pltpu.VMEM((GROUPS, MEM * VB, 512), jnp.bfloat16),
            pltpu.VMEM((GROUPS, MEM * VB, 3 * LANE), jnp.float32),
            pltpu.VMEM((GROUPS, 8, 3 * LANE), jnp.float32),
            pltpu.VMEM((LANE, LANE), jnp.float32),
        ],
        compiler_params=pltpu.CompilerParams(vmem_limit_bytes=20 * mib),
        cost_estimate=pl.CostEstimate(flops=6 * 10**9, bytes_accessed=5 * 10**6, transcendentals=5 * 10**6),
        name="score",
    )(got, legendre)
    got = lax.all_to_all(sent, MESH_AXES, 0, 0, tiled=True)

    grid_grad, coef_score = pl.pallas_call(
        inverse_kernel,
        in_specs=[vmem_spec, vmem_spec],
        out_specs=[any_spec, vmem_spec],
        out_shape=[
            jax.ShapeDtypeStruct((1, 12, 64, NLON), jnp.bfloat16),
            jax.ShapeDtypeStruct((10, 20), jnp.float32),
        ],
        scratch_shapes=[
            pltpu.VMEM((4096, LANE), jnp.float32),
            pltpu.VMEM((1, 12, 64, NLON), jnp.bfloat16),
            pltpu.SemaphoreType.DMA((2,)),
        ],
        compiler_params=pltpu.CompilerParams(vmem_limit_bytes=24 * mib),
        cost_estimate=pl.CostEstimate(flops=2 * 10**9, bytes_accessed=4 * 10**6, transcendentals=0),
        name="inverse",
    )(got, table)
    return (grid_grad.transpose(0, 2, 1, 3), coef_score)


def solution(mesh):
    placed = (P("ens", None, "lat", None), P(None, "lat", None), P())
    return jax.shard_map(
        body,
        mesh=mesh,
        in_specs=placed,
        out_specs=(P("ens", None, "lat", None), P("lat", "ens")),
        check_vma=False,
    )
```

```python
import math

import jax
import jax.numpy as jnp
import numpy as np
from jax import lax
from jax.experimental import pallas as pl
from jax.experimental.pallas import tpu as pltpu
from jax.sharding import PartitionSpec as P

SOFT2 = 0.1 * 0.1
CEILING = 2.0**60
SHRINK = 2.0 ** (-60)
LOG_SHIFT = 60.0 * math.log(2.0)
NLON, NLAT, DEG, MEM = 720, 384, 320, 16
GROUPS, VB = 5, 16
LANE = 128
MESH_AXES = ("ens", "lat")


def message_order(columns):
    row = lax.broadcasted_iota(jnp.int32, (LANE, LANE), 0)
    lane = lax.broadcasted_iota(jnp.int32, (LANE, LANE), 1)
    k, ahead = (row >> 4) & 3, (row & 15) - lane + 256 * (row >> 6)
    groups = []
    for g in range(GROUPS):
        extra = 80 if g < 3 else 160
        place = ahead + 16 * g + jnp.where(k < 2, k * LANE, jnp.where(k == 2, extra, -2048))
        tiles = [jnp.where(place == q * LANE, 1.0, 0.0) for q in range(columns)]
        groups.append(jnp.concatenate(tiles, axis=1).astype(jnp.bfloat16))
    return groups


def latitude_order():
    row = np.arange(256)
    jb, c = row // 8, row % 8
    return np.concatenate([12 * jb + c, 12 * jb + 8 + c // 2])


def dot(a, b, dims=((1,), (0,))):
    return lax.dot_general(a, b, (dims, ((), ())), preferred_element_type=jnp.float32)


STEP = math.pi / 360.0
SIN_TERMS = [(-1) ** n / math.factorial(2 * n + 1) * STEP ** (2 * n + 1) / math.sqrt(NLON) for n in range(6)]


def scaled_sine(steps):
    square = steps * steps
    total = SIN_TERMS[5]
    for term in SIN_TERMS[4::-1]:
        total = total * square + term
    return (total * steps).astype(jnp.bfloat16)


def fourier_blocks(wave):
    lon = lax.broadcasted_iota(jnp.int32, (32, NLON), 1).astype(jnp.float32)
    turn = wave * lon
    turn = turn - NLON * jnp.floor((turn + 0.5) * (1.0 / NLON)) - 360.0
    folded = jnp.maximum(jnp.minimum(turn, 360.0 - turn), -360.0 - turn)
    return scaled_sine(jnp.abs(turn) - 180.0), scaled_sine(folded)


def forward_kernel(
    wave_ref, members_hbm, analysis_hbm, sent_hbm, table_hbm, members, analysis, rows, sent_ref, table_ref, sems
):
    loads = [
        pltpu.make_async_copy(members_hbm, members, sems.at[0]),
        pltpu.make_async_copy(analysis_hbm, analysis, sems.at[1]),
    ]
    for load in loads:
        load.start()
    waves = jnp.broadcast_to(wave_ref[...].reshape(1, DEG).astype(jnp.float32), (32, DEG))
    ahead = lax.broadcasted_iota(jnp.int32, (32, DEG), 1) - 10 * lax.broadcasted_iota(jnp.int32, (32, DEG), 0)
    columns = [jnp.sum(jnp.where(ahead == k, waves, 0.0), axis=1, keepdims=True) for k in range(10)]
    for slot in range(10):
        for part, block in enumerate(fourier_blocks(columns[slot])):
            sb, g = divmod(2 * slot + part, GROUPS)
            at = g * LANE + sb * 32
            table_ref[at : at + 32, :] = block
    stores = [pltpu.make_async_copy(table_ref, table_hbm, sems.at[2])]
    stores[0].start()
    order = jnp.concatenate(message_order(4), axis=0)
    for load in loads:
        load.wait()

    deviation = (members[0].astype(jnp.float32) - analysis[...].astype(jnp.float32)).astype(
        jnp.bfloat16
    )
    blank = jnp.zeros((VB, NLON), jnp.bfloat16)
    for h in range(2):
        pieces = []
        for t in range(4):
            for vb in (2 * h, 2 * h + 1):
                pieces += [deviation[j, vb * VB : (vb + 1) * VB] for j in (2 * t, 2 * t + 1, 8 + t)] + [blank]
        fourier = dot(table_ref[...], jnp.concatenate(pieces, axis=0), ((1,), (1,))).astype(jnp.bfloat16)
        wide = jnp.concatenate(
            [
                jnp.concatenate(
                    [fourier[g * LANE : (g + 1) * LANE, t * LANE : (t + 1) * LANE] for g in range(GROUPS)],
                    axis=1,
                )
                for t in range(4)
            ],
            axis=0,
        )
        placed = dot(wide, order)
        for t in range(4):
            for q in range(4):
                at = (q // 2) * LANE * 8 + 2 * t + q % 2
                rows[h, pl.ds(at, LANE, stride=8), :] = placed[
                    t * LANE : (t + 1) * LANE, q * LANE : (q + 1) * LANE
                ]
        sent_ref[h * 256 : (h + 1) * 256] = rows[h].reshape(256, 8, LANE).astype(jnp.bfloat16)
        half = pl.ds(h * 256, 256)
        stores.append(pltpu.make_async_copy(sent_ref.at[half], sent_hbm.at[half], sems.at[3 + h]))
        stores[-1].start()
    for store in stores:
        store.wait()


def legendre_kernel(wave_ref, base_ref, cos_ref, logsin_ref, weight_ref, leg_ref, rows):
    wave = jnp.broadcast_to(wave_ref[...], (8, 512))
    wave2 = wave * wave
    cosine = jnp.broadcast_to(cos_ref[...], (8, 512))
    weight = jnp.broadcast_to(weight_ref[...], (8, 512))
    start_log = base_ref[...] + wave * logsin_ref[...]
    zero = jnp.zeros((8, 512), jnp.float32)

    def block(b, carry):
        for offset in range(8):
            previous, older, inverse, log_scale = carry
            index = b * 8 + offset
            degree = index.astype(jnp.float32)
            square = jnp.full((8, 512), degree * degree, jnp.float32)
            ratio = jnp.maximum(square - wave2, 1.0) / jnp.maximum(4.0 * square - 1.0, 1.0)
            factor = lax.rsqrt(ratio)
            current = factor * (cosine * previous - older * inverse)
            current = jnp.where(wave == degree, 1.0, current)
            too_large = jnp.abs(current) > CEILING
            shrink = jnp.where(too_large, SHRINK, 1.0)
            log_scale = jnp.where(too_large, log_scale + LOG_SHIFT, log_scale)
            current = current * shrink
            previous = previous * shrink
            value = weight * (current * jnp.exp(log_scale))
            for q in range(4):
                rows[q, pl.ds(pl.multiple_of(index * 8, 8), 8), :] = value[:, q * LANE : (q + 1) * LANE]
            carry = (current, previous, ratio * factor, log_scale)
        return carry

    lax.fori_loop(0, DEG // 8, block, (zero, zero, zero + 1.0, start_log))
    for s in range(3):
        for q in range(4):
            part = rows[q, pl.ds(s, DEG, stride=8), :]
            at = s * 512 + q * LANE
            leg_ref[:, at : at + LANE] = part.astype(jnp.bfloat16)


def pair_terms(z):
    pull = [None] * MEM
    inverse_sum = None
    for a in range(MEM):
        for b in range(a + 1, MEM):
            diff = z[a] - z[b]
            inverse = lax.rsqrt(diff * diff + SOFT2)
            term = diff * inverse
            inverse_sum = inverse if inverse_sum is None else inverse_sum + inverse
            pull[a] = term if pull[a] is None else pull[a] + term
            pull[b] = -term if pull[b] is None else pull[b] - term
    pair_abs = SOFT2 * inverse_sum
    single = None
    grads = []
    for e in range(MEM):
        square = z[e] * z[e] + SOFT2
        inverse = lax.rsqrt(square)
        soft = square * inverse
        single = soft if single is None else single + soft
        pair_abs = pair_abs + z[e] * pull[e]
        grads.append(z[e] * inverse - pull[e] * (1.0 / (MEM - 1)))
    pairs = MEM * (MEM - 1)
    return grads, (single - 0.1 * MEM) * (1.0 / MEM) - (pair_abs - 0.1 * (pairs // 2)) * (1.0 / pairs)


def score_kernel(got_ref, leg_ref, sent_ref, turned, coef, sums, scores):
    own_lat = lax.axis_index("lat")
    odd_block = lax.rem(lax.axis_index("ens"), 2)
    even = lax.broadcasted_iota(jnp.int32, (48, 256), 1) & 1 == 0
    unit = lax.broadcasted_iota(jnp.int32, (256, 256), 0) == lax.broadcasted_iota(jnp.int32, (256, 256), 1)
    unit = jnp.where(unit, 1.0, 0.0).astype(jnp.bfloat16)

    def slot_lanes(g):
        return pl.ds(pl.multiple_of((g + odd_block) // 2 * 512, 512), 512)

    def turn(pair, _):
        messages = []
        for k in range(2):
            message = got_ref[pl.ds(pl.multiple_of((2 * pair + k) * 32, 32), 32)].astype(jnp.float32)
            messages.append(message.reshape(256, LANE).astype(jnp.bfloat16))
        both = dot(unit, jnp.concatenate(messages, axis=1), ((1,), (1,)))
        for k in range(2):
            rows = both[k * LANE : (k + 1) * LANE]
            at = pl.ds(pl.multiple_of((2 * pair + k) * VB, VB), VB)
            low = jnp.where(even, rows[80:128], 0.0).astype(jnp.bfloat16)
            high = jnp.where(even, 0.0, rows[80:128]).astype(jnp.bfloat16)
            for g in range(GROUPS):
                turned[g, at, 0:256] = rows[g * VB : (g + 1) * VB].astype(jnp.bfloat16)
                extra = low[g * VB : (g + 1) * VB] if g < 3 else high[(g - 3) * VB : (g - 2) * VB]
                turned[g, at, 256:512] = extra
        return 0

    lax.fori_loop(0, MEM // 2, turn, 0, unroll=True)

    first_half = lax.broadcasted_iota(jnp.int32, (8, LANE), 1) < 64

    def spectra(g):
        values = dot(turned[g], leg_ref[:, slot_lanes(g)], ((1,), (1,)))
        coef[g, :, 0:DEG] = values.astype(jnp.bfloat16).astype(jnp.float32)

    def score(g):
        for q in range(2):
            lanes = slice(q * LANE, (q + 1) * LANE)
            total = None
            for r in range(2):
                rows = [slice(e * VB + r * 8, e * VB + r * 8 + 8) for e in range(MEM)]
                grads, per = pair_terms([coef[g, row, lanes] for row in rows])
                for row, grad in zip(rows, grads):
                    coef[g, row, lanes] = grad
                total = per if total is None else total + per
            sums[g, :, lanes] = total
        lanes = slice(2 * LANE, 3 * LANE)
        packed = []
        for e in range(MEM):
            top, bottom = coef[g, e * VB : e * VB + 8, lanes], coef[g, e * VB + 8 : e * VB + VB, lanes]
            packed.append(jnp.where(first_half, top, pltpu.roll(bottom, 64, 1)))
        grads, per = pair_terms(packed)
        for e in range(MEM):
            coef[g, e * VB : e * VB + 8, lanes] = grads[e]
            coef[g, e * VB + 8 : e * VB + VB, lanes] = pltpu.roll(grads[e], 64, 1)
        sums[g, :, lanes] = per + pltpu.roll(per, 64, 1)

    def gradient(g):
        grad = coef[g, :, 0:DEG].astype(jnp.bfloat16)
        turned[g] = dot(grad, leg_ref[:, slot_lanes(g)]).astype(jnp.bfloat16)

    spectra(0)
    for g in range(GROUPS):
        if g + 1 < GROUPS:
            spectra(g + 1)
        score(g)
        gradient(g)

    place = lax.broadcasted_iota(jnp.int32, (16, DEG), 0)
    same = lax.rem(lax.broadcasted_iota(jnp.int32, (16, DEG), 1), 5) == lax.rem(place, 5)
    spread = jnp.zeros((16, DEG), jnp.float32)
    for g in range(GROUPS):
        mine = same & (place < 15) & (place // 5 == (g + odd_block) // 2)
        own = jnp.sum(sums[g], axis=0, keepdims=True)[:, 0:DEG]
        spread = spread + jnp.where(mine, jnp.broadcast_to(own, (16, DEG)), 0.0)
    spread = jnp.concatenate([jnp.zeros((112, DEG), jnp.float32), spread], axis=0).astype(jnp.bfloat16)
    out_row = lax.broadcasted_iota(jnp.int32, (LANE, DEG), 0)
    out_deg = lax.broadcasted_iota(jnp.int32, (LANE, DEG), 1)
    pick = (lax.rem(out_row, 2) == 1) & (out_deg // 5 == (out_row // 8) * 4 + lax.rem(out_row, 8) // 2)
    scores[...] = dot(jnp.where(pick, 1.0, 0.0).astype(jnp.bfloat16), spread, ((1,), (1,)))

    def send(pair, _):
        rows = []
        for k in range(2):
            at = pl.ds(pl.multiple_of((2 * pair + k) * VB, VB), VB)
            rows += [turned[g, at, 0:256] for g in range(GROUPS)]
            extra = [turned[g, at, 256:512].astype(jnp.float32) for g in range(GROUPS)]
            blank = jnp.zeros((VB, 256), jnp.float32)
            extra = jnp.where(even, jnp.concatenate(extra[:3]), jnp.concatenate(extra[3:] + [blank]))
            rows.append(extra.astype(jnp.bfloat16))
        back = dot(unit, jnp.concatenate(rows, axis=0), ((1,), (1,)))
        for k in range(2):
            member = 2 * pair + k
            message = back[:, k * LANE : (k + 1) * LANE].reshape(32, 8, LANE)
            sent_ref[pl.ds(pl.multiple_of(member * 32, 32), 32)] = message.astype(jnp.bfloat16)
            part = scores[pl.ds(pl.multiple_of(member * 8, 8), 8), :]
            own = member * 32 + own_lat
            sent_ref[own] = (sent_ref[own].astype(jnp.float32) + part).astype(jnp.bfloat16)
        return 0

    lax.fori_loop(0, MEM // 2, send, 0, unroll=True)


def inverse_kernel(got_ref, table_ref, grid_hbm, score_ref, rows, grid, sems):
    own_lat = lax.axis_index("lat")
    order = jnp.concatenate([group[0:48] for group in message_order(2)], axis=0)
    rows[...] = got_ref[...].astype(jnp.float32).reshape(512 * 8, LANE)
    turned = []
    for t in range(4):
        pair = [rows[pl.ds(2 * t + c, 512, stride=8), :].astype(jnp.bfloat16) for c in range(2)]
        turned.append(dot(order, jnp.concatenate(pair, axis=1), ((1,), (1,))).astype(jnp.bfloat16))
    left = []
    for vb in range(4):
        for t in range(4):
            tiles = [turned[t][g * 48 : (g + 1) * 48, vb * LANE : (vb + 1) * LANE] for g in range(GROUPS)]
            left.append(jnp.concatenate(tiles, axis=1))
    result = dot(jnp.concatenate(left, axis=0), table_ref[...]).astype(jnp.bfloat16)
    stores = []
    for h in range(2):
        for vb in (2 * h, 2 * h + 1):
            for t in range(4):
                for k, j in enumerate((2 * t, 2 * t + 1, 8 + t)):
                    at = (vb * 4 + t) * 48 + k * VB
                    grid[0, j, vb * VB : (vb + 1) * VB, :] = result[at : at + VB]
        half = (slice(None), slice(None), slice(h * 32, (h + 1) * 32), slice(None))
        stores.append(pltpu.make_async_copy(grid.at[half], grid_hbm.at[half], sems.at[h]))
        stores[-1].start()

    slot = lax.broadcasted_iota(jnp.int32, (16, LANE), 0)
    column = lax.broadcasted_iota(jnp.int32, (16, LANE), 1) - 112
    parts = [None] * 4
    for sb in range(4):
        tile = None
        for vb in range(4):
            piece = rows[pl.ds(pl.multiple_of((vb * LANE + sb * 32 + own_lat) * 8, 8), 8), :]
            tile = piece if tile is None else tile + piece
        here = (column >= 0) & (slot == (5 * sb) // 2 + (column + 5) // 5 - 1)
        for t in range(4):
            spread = jnp.where(here, jnp.broadcast_to(tile[2 * t + 1 : 2 * t + 2], (16, LANE)), 0.0)
            parts[t] = spread if parts[t] is None else parts[t] + spread
    source = lax.broadcasted_iota(jnp.int32, (512, LANE), 0)
    target = lax.broadcasted_iota(jnp.int32, (512, LANE), 1)
    inside = source % LANE - 110
    fits = (inside >= 2) & (inside < 17) & (target == 5 * (source // LANE) + (inside + 3) % 5)
    scores = lax.dot_general(
        jnp.concatenate(parts, axis=1),
        jnp.where(fits, 1.0, 0.0),
        (((1,), (0,)), ((), ())),
        precision=lax.Precision.HIGHEST,
        preferred_element_type=jnp.float32,
    )
    score_ref[...] = scores[:10, :20] * (1.0 / 128)
    for store in stores:
        store.wait()


def body(members, analysis, wave_order):
    mib = 1 << 20
    any_spec = pl.BlockSpec(memory_space=pltpu.HBM)
    vmem_spec = pl.BlockSpec(memory_space=pltpu.VMEM)
    waves = wave_order.astype(jnp.float32)
    sent, table = pl.pallas_call(
        forward_kernel,
        in_specs=[vmem_spec, any_spec, any_spec],
        out_specs=[any_spec, any_spec],
        out_shape=[
            jax.ShapeDtypeStruct((512, 8, LANE), jnp.bfloat16),
            jax.ShapeDtypeStruct((640, NLON), jnp.bfloat16),
        ],
        scratch_shapes=[
            pltpu.VMEM((1, 12, 64, NLON), jnp.bfloat16),
            pltpu.VMEM((12, 64, NLON), jnp.bfloat16),
            pltpu.VMEM((2, 2048, LANE), jnp.float32),
            pltpu.VMEM((512, 8, LANE), jnp.bfloat16),
            pltpu.VMEM((640, NLON), jnp.bfloat16),
            pltpu.SemaphoreType.DMA((5,)),
        ],
        compiler_params=pltpu.CompilerParams(vmem_limit_bytes=60 * mib),
        cost_estimate=pl.CostEstimate(flops=3 * 10**9, bytes_accessed=4 * 10**6, transcendentals=0),
        name="forward",
    )(wave_order, members.transpose(0, 2, 1, 3), analysis.transpose(1, 0, 2))
    got = lax.all_to_all(sent, MESH_AXES, 0, 0, tiled=True)

    own = lax.axis_index("lat") * 10 + (5 * lax.rem(lax.axis_index("ens"), 4)) // 2
    slots = lax.dynamic_slice_in_dim(waves, own, 3)
    slots = jnp.concatenate([slots, jnp.broadcast_to(slots[2:3], (5,))]).reshape(8, 1)
    base = 0.5 * (
        lax.lgamma(slots + 1.5) - lax.lgamma(slots + 1.0) - lax.lgamma(jnp.float32(1.5)) + math.log(0.5)
    )
    colatitude = (latitude_order() + 0.5) * (math.pi / NLAT)
    constants = [np.cos(colatitude), np.log(np.sin(colatitude)), math.sqrt(math.pi / NLAT) * np.sin(colatitude)]
    constants = [jnp.asarray(c[None].astype(np.float32)) for c in constants]
    legendre = pl.pallas_call(
        legendre_kernel,
        out_shape=jax.ShapeDtypeStruct((DEG, 1536), jnp.bfloat16),
        scratch_shapes=[pltpu.VMEM((4, DEG * 8, LANE), jnp.float32)],
        compiler_params=pltpu.CompilerParams(vmem_limit_bytes=16 * mib),
        cost_estimate=pl.CostEstimate(flops=10**8, bytes_accessed=2 * 10**6, transcendentals=3 * 10**6),
        name="legendre",
    )(slots, base, *constants)

    sent = pl.pallas_call(
        score_kernel,
        out_shape=jax.ShapeDtypeStruct((512, 8, LANE), jnp.bfloat16),
        scratch_shapes=[
            pltpu.VMEM((GROUPS, MEM * VB, 512), jnp.bfloat16),
            pltpu.VMEM((GROUPS, MEM * VB, 3 * LANE), jnp.float32),
            pltpu.VMEM((GROUPS, 8, 3 * LANE), jnp.float32),
            pltpu.VMEM((LANE, LANE), jnp.float32),
        ],
        compiler_params=pltpu.CompilerParams(vmem_limit_bytes=20 * mib),
        cost_estimate=pl.CostEstimate(flops=6 * 10**9, bytes_accessed=5 * 10**6, transcendentals=5 * 10**6),
        name="score",
    )(got, legendre)
    got = lax.all_to_all(sent, MESH_AXES, 0, 0, tiled=True)

    grid_grad, coef_score = pl.pallas_call(
        inverse_kernel,
        in_specs=[vmem_spec, vmem_spec],
        out_specs=[any_spec, vmem_spec],
        out_shape=[
            jax.ShapeDtypeStruct((1, 12, 64, NLON), jnp.bfloat16),
            jax.ShapeDtypeStruct((10, 20), jnp.float32),
        ],
        scratch_shapes=[
            pltpu.VMEM((4096, LANE), jnp.float32),
            pltpu.VMEM((1, 12, 64, NLON), jnp.bfloat16),
            pltpu.SemaphoreType.DMA((2,)),
        ],
        compiler_params=pltpu.CompilerParams(vmem_limit_bytes=24 * mib),
        cost_estimate=pl.CostEstimate(flops=2 * 10**9, bytes_accessed=4 * 10**6, transcendentals=0),
        name="inverse",
    )(got, table)
    return (grid_grad.transpose(0, 2, 1, 3), coef_score)


def solution(mesh):
    placed = (P("ens", None, "lat", None), P(None, "lat", None), P())
    return jax.shard_map(
        body,
        mesh=mesh,
        in_specs=placed,
        out_specs=(P("ens", None, "lat", None), P("lat", "ens")),
        check_vma=False,
    )
```
